256 devices in a mesh: ia: 8 (over z), ja: 32 (over x, y, core).
Axes of the slice: x: 4, y: 4, z: 8, core: 2. Of those that a mesh axis runs over, the one named last changes fastest.
Arguments:
- tensor: float32 [8, 8192, 8192], P(None, 'ia', 'ja'), may hold values from -6 to 6
- factor_b: float32 [8192, 256], P(('ja', 'ia')), may hold values from -24 to 24, as said below
- factor_c: float32 [8, 256], replicated, may hold values from -0.0234375 to 0.0234375
Outputs:
- factor_a: float32 [8192, 256], P(('ia', 'ja'))
- factor_b_new: float32 [8192, 256], P(('ja', 'ia'))
The draws below stay inside these ranges and needn't reach their ends.
Inputs may be any that keep to these rules, and one draw needn't show every extreme that they name: `factor_b`: real-valued entries.
All inputs are finite; a program needn't handle non-finite values.
Results may differ from the reference program's by a relative error of at most 0.0001.
Values sent between devices are 32-bit elements; how exact they have to be, the bound alone decides.
A program may use at most 64 MiB of HBM per device.

```python
import math
import jax
import jax.numpy as jnp
from jax import lax

K = 8
R = 256
I = 8192
J = 8192


def draw_factor_b(key, part):
    key = jax.random.fold_in(key, 7)
    first, second, third = jax.random.split(key, 3)
    rise = 1.0 + 2.0 * jnp.arange(J, dtype=jnp.float32)[:, None] / J
    base = jnp.clip(jax.random.normal(first, (J, R), jnp.float32), -4.0, 4.0)
    scales = jnp.exp(jax.random.uniform(second, (J, 1), jnp.float32, 0.0, math.log(10.0))) / 10.0
    columns = jnp.exp(jax.random.uniform(third, (1, R), jnp.float32, math.log(0.5), math.log(2.0)))
    return base * scales * rise * columns


def with_spikes(array, stream_key, source, target, blocks, factor):
    owner, partner = [(jnp.arange(array.shape[dim]) // (array.shape[dim] // blocks)).reshape([-1 if axis == dim else 1 for axis in range(array.ndim)]) for dim in (source, target)]
    chosen = jax.random.permutation(stream_key, blocks)[partner]
    strong = (owner == chosen) | (owner == (partner + blocks // 2) % blocks)
    return jnp.where(strong, factor * array, array)


def shard_levels(rng, shape, pieces, smallest, high):
    def one(axis_at, parts):
        draws = jax.random.uniform(jax.random.fold_in(jax.random.fold_in(rng, 6), axis_at), (parts,), jnp.float32, smallest / len(pieces), high / len(pieces))
        return jnp.repeat(jnp.exp(draws), shape[axis_at] // parts).reshape((-1,) + (1,) * (len(shape) - axis_at - 1))

    level = one(*pieces[0])
    for cut in pieces[1:]:
        level = level * one(*cut)
    return level


def bell_draw(stream_key, extent, deviation, most, cuts=(), kind=jnp.bfloat16):
    array = jax.random.normal(stream_key, extent, jnp.float32) * deviation
    if len(cuts) > 0:
        array = shard_levels(stream_key, extent, cuts, -0.22, 0.18) * array
    return jnp.clip(array, min=-most, max=most).astype(kind)


def bell_draw_with(rng, extent, spread, reach, shards, heavy, held_as=jnp.bfloat16):
    entries = spread * jax.random.normal(rng, extent, jnp.float32)
    if shards:
        entries = entries * shard_levels(rng, extent, shards, -0.22, 0.18)
    return jnp.clip(with_spikes(entries, jax.random.fold_in(rng, 3), *heavy), -reach, reach).astype(held_as)


def setup_inputs(seed: int = 0) -> dict:
    splits = jax.random.split(jax.random.key(seed), 4)
    tensor = bell_draw_with(splits[0], (K, I, J), 1.0, 6.0, ((1, 8), (2, 32)), (2, 1, 32, 2.75), jnp.float32)
    factor_b = draw_factor_b(jax.random.fold_in(splits[3], 71), 0)
    factor_c = bell_draw(splits[2], (K, R), 0.00390625, 0.0234375, (), jnp.float32)
    return dict(tensor=tensor, factor_b=factor_b, factor_c=factor_c)


RIDGE = 0.001

def cross(left, right):
    return lax.dot_general(left.astype(jnp.float32), right.astype(jnp.float32), (((0,), (0,)), ((), ())), precision=lax.Precision.HIGHEST, preferred_element_type=jnp.float32)

def solve_rows(moments, gram_c, gram_other):
    size = gram_c.shape[0]
    system = gram_c * gram_other + RIDGE * jnp.eye(size, dtype=jnp.float32)
    lower = jnp.linalg.cholesky(system)
    middle = lax.linalg.triangular_solve(lower, moments, left_side=False, lower=True, transpose_a=True)
    return lax.linalg.triangular_solve(lower, middle, left_side=False, lower=True, transpose_a=False)

def reference(tensor, factor_b, factor_c):
    highest = lax.Precision.HIGHEST
    gram_c = cross(factor_c, factor_c)
    gram_b = cross(factor_b, factor_b)
    moments_a = jnp.zeros((tensor.shape[1], factor_c.shape[1]), jnp.float32)
    for layer in range(tensor.shape[0]):
        moments_a = moments_a + jnp.dot(tensor[layer].astype(jnp.float32), (factor_b * factor_c[layer][None, :]).astype(jnp.float32), precision=highest, preferred_element_type=jnp.float32)
    factor_a = solve_rows(moments_a, gram_c, gram_b)
    gram_a = cross(factor_a, factor_a)
    moments_b = jnp.zeros((tensor.shape[2], factor_c.shape[1]), jnp.float32)
    for layer in range(tensor.shape[0]):
        moments_b = moments_b + cross(tensor[layer], factor_a * factor_c[layer][None, :])
    factor_b_new = solve_rows(moments_b, gram_c, gram_a)
    return (factor_a, factor_b_new)
```

```python
import functools

import jax
import jax.numpy as jnp
from jax import lax
from jax.experimental import pallas as pl
from jax.experimental.pallas import tpu as pltpu
from jax.sharding import PartitionSpec as P

RIDGE = 0.001
MESH = pl.DeviceIdType.MESH
F32 = jnp.float32
BF16 = jnp.bfloat16
PB = 16
CHUNKS = 4


def split2(x):
    high = x.astype(BF16)
    return high, (x - high.astype(F32)).astype(BF16)


def split3(x):
    high = x.astype(BF16)
    rest = x - high.astype(F32)
    mid = rest.astype(BF16)
    return high, mid, (rest - mid.astype(F32)).astype(BF16)


def cross(left, right):
    lh, lm, ll = split3(left)
    rh, rm, rl = split3(right)
    a = jnp.concatenate([lh, lh, lm, lh, lm, ll], axis=0)
    b = jnp.concatenate([rh, rm, rh, rl, rm, rh], axis=0)
    return lax.dot_general(a, b, (((0,), (0,)), ((), ())), preferred_element_type=F32)


def row_of(block, at):
    return jnp.broadcast_to(block[at : at + 1, :], block.shape)


def sweep_small(cols, width):
    row = lax.broadcasted_iota(jnp.int32, (8, width), 0)
    halves = range(PB // 8)
    for j in range(0, PB, 2):
        h, jj = j // 8, j % 8
        u0, u1 = cols[j], cols[j + 1]
        first, second = row == jj, row == jj + 1
        a, b, d = row_of(u0[h], jj), row_of(u0[h], jj + 1), row_of(u1[h], jj + 1)
        scale = 1.0 / (a * d - b * b)
        p00, p01, p11 = d * scale, -b * scale, a * scale
        fresh = []
        for l in range(PB):
            if l == j or l == j + 1:
                r0, r1 = (p00, p01) if l == j else (p01, p11)
                col = [u0[g] * r0 + u1[g] * r1 for g in halves]
                r0, r1 = -r0, -r1
            else:
                q0, q1 = row_of(cols[l][h], jj), row_of(cols[l][h], jj + 1)
                r0, r1 = p00 * q0 + p01 * q1, p01 * q0 + p11 * q1
                col = [cols[l][g] - u0[g] * r0 - u1[g] * r1 for g in halves]
            col[h] = jnp.where(first, r0, jnp.where(second, r1, col[h]))
            fresh.append(col)
        cols = fresh
    return cols


def sweep(s_ref):
    size = s_ref.shape[0]
    lanes = lax.broadcasted_iota(jnp.int32, (PB, size), 1)
    rows = lax.broadcasted_iota(jnp.int32, (PB, size), 0)
    width = 128

    def step(k, carry):
        at = pl.multiple_of(k * PB, PB)
        panel = s_ref[pl.ds(at, PB), :]
        cols = []
        for l in range(PB):
            col = jnp.sum(jnp.where(lanes == at + l, panel, 0.0), axis=1, keepdims=True)
            col = jnp.broadcast_to(col, (PB, width))
            cols.append([col[8 * g : 8 * g + 8] for g in range(PB // 8)])
        cols = sweep_small(cols, width)
        inside = (lanes >= at) & (lanes < at + PB)
        source = jnp.where(inside, jnp.where(lanes == at + rows, 1.0, 0.0), -panel)
        parts = [[None] * (size // width) for _ in range(PB // 8)]
        for l in range(PB):
            for w in range(size // width):
                line = jnp.broadcast_to(source[l : l + 1, w * width : (w + 1) * width], (8, width))
                for g in range(PB // 8):
                    term = cols[l][g] * line
                    parts[g][w] = term if l == 0 else parts[g][w] + term
        fresh = jnp.concatenate([jnp.concatenate(p, axis=1) for p in parts], axis=0)
        update = cross(panel, fresh)
        whole = lax.broadcasted_iota(jnp.int32, (size, size), 1)
        kept = jnp.where((whole >= at) & (whole < at + PB), 0.0, s_ref[...])
        s_ref[...] = kept - update
        s_ref[pl.ds(at, PB), :] = fresh
        return carry

    lax.fori_loop(0, size // PB, step, 0)


def dot(a, b):
    return jnp.dot(a, b, preferred_element_type=F32)


def full_dot(a, b):
    return jnp.dot(a, b, precision=lax.Precision.HIGHEST, preferred_element_type=F32)


def kernel(nz, nj, t_hbm, b_ref, c_ref, fa_ref, fb_ref,
           t_f32, t_hi, t_lo, w_hi, w_lo, b_all, c_pad, c_turn, gram_c,
           gram, g1, g1_sum, g2, g2_sum, g3, system,
           tot, sib, comb, landed, a_all, at_hi, at_lo, tot_b, h_land,
           t_sem, a_s, a_r, g1_s, g1_r, g2_s, g2_r, g3_s, g3_r, c1_s, c1_r, c2_s, c2_r, e1_s, e2_s, e_r, h_s, h_r):
    z, p = lax.axis_index("ia"), lax.axis_index("ja")
    q, c = p // 2, p % 2
    nq = nj // 2
    per = b_ref.shape[0]
    rank = b_ref.shape[1]
    layers = t_hbm.shape[0]
    high = t_hbm.shape[1]
    wide = t_hbm.shape[2]
    slab = rank // nj
    other = p + 1 - 2 * c

    def send(src, dst, s_sem, r_sem, to):
        return pltpu.make_async_remote_copy(
            src_ref=src, dst_ref=dst, send_sem=s_sem, recv_sem=r_sem, device_id=to, device_id_type=MESH
        )

    def each(n, body):
        lax.fori_loop(0, n, lambda s, carry: (body(s), carry)[1], 0)

    t_copies = [pltpu.make_async_copy(t_hbm.at[k], t_f32.at[k], t_sem.at[k]) for k in range(layers)]
    for copy in t_copies:
        copy.start()

    barrier = pltpu.get_barrier_semaphore()
    each(nj - 1, lambda s: pl.semaphore_signal(
        barrier, inc=1, device_id=(z, (p + 1 + s) % nj), device_id_type=MESH))
    each(nz - 1, lambda s: pl.semaphore_signal(
        barrier, inc=1, device_id=((z + 1 + s) % nz, p), device_id_type=MESH))

    def g1_copy(t, to, slot):
        return send(gram.at[t, to], g1.at[t, slot], g1_s.at[t, to], g1_r.at[t, slot], (z, to))

    def g2_copy(t, to, slot):
        return send(g1_sum.at[t], g2.at[t, slot], g2_s.at[t, to], g2_r.at[t, slot], (to, p))

    def g3_copy(t, to, slot):
        return send(g2_sum.at[t], g3.at[t, slot], g3_s.at[t, to], g3_r.at[t, slot], (z, to))

    def gram_local(t, rows):
        gram[t] = cross(rows, rows).reshape(nj, slab, rank)

    def gram_1(t):
        each(nj - 1, lambda s: g1_copy(t, (p + 1 + s) % nj, p).start())

    def gram_2(t):
        g1[t, p] = gram[t, p]
        each(nj - 1, lambda s: g1_copy(t, p, (p + 1 + s) % nj).wait_recv())
        total = g1[t, 0]
        for s in range(1, nj):
            total = total + g1[t, s]
        g1_sum[t] = total
        each(nz - 1, lambda s: g2_copy(t, (z + 1 + s) % nz, z).start())
        g2[t, z] = total

    def gram_3(t):
        each(nz - 1, lambda s: g2_copy(t, z, (z + 1 + s) % nz).wait_recv())
        total = g2[t, 0]
        for s in range(1, nz):
            total = total + g2[t, s]
        g2_sum[t] = total
        each(nj - 1, lambda s: g3_copy(t, (p + 1 + s) % nj, p).start())
        g3[t, p] = total

    def gram_4(t):
        each(nj - 1, lambda s: g3_copy(t, p, (p + 1 + s) % nj).wait_recv())
        rows = lax.broadcasted_iota(jnp.int32, (rank, rank), 0)
        lanes = lax.broadcasted_iota(jnp.int32, (rank, rank), 1)
        value = gram_c[...] * g3[t].reshape(rank, rank)
        system[...] = value + jnp.where(rows == lanes, RIDGE, 0.0)
        sweep(system)

    gram_local(0, b_ref[...])
    pl.semaphore_wait(barrier, nj - 1 + nz - 1)

    def a_copy(to, slot):
        return send(b_ref, b_all.at[slot], a_s.at[to], a_r.at[slot], (to, p))

    gram_1(0)
    each(nz - 1, lambda s: a_copy((z + 1 + s) % nz, z).start())
    b_all[z] = b_ref[...]

    c_pad[...] = jnp.zeros_like(c_pad)
    c_pad[0:layers, :] = c_ref[...]
    gram_c[...] = cross(c_pad[0:16, :], c_pad[0:16, :])
    c_turn[...] = c_pad[...].T

    strip = min(256, high)
    for k in range(layers):
        t_copies[k].wait()

        def convert(s, k=k):
            at = pl.multiple_of(s * strip, strip)
            hi, lo = split2(t_f32[k, pl.ds(at, strip), :])
            t_hi[pl.ds(at, strip), k * wide : (k + 1) * wide] = hi
            t_lo[pl.ds(at, strip), k * wide : (k + 1) * wide] = lo

        each(high // strip, convert)

    gram_2(0)

    each(nz - 1, lambda s: a_copy(z, (z + 1 + s) % nz).wait_recv())
    rows_b = b_all[...].reshape(wide, rank)
    for k in range(layers):
        hi, lo = split2(rows_b * c_ref[k : k + 1, :])
        w_hi[k * wide : (k + 1) * wide, :] = hi
        w_lo[k * wide : (k + 1) * wide, :] = lo

    group = nq // CHUNKS

    def c1_copy(chip):
        return send(tot.at[chip, 1 - c], sib.at[chip], c1_s.at[chip], c1_r.at[chip], (z, other))

    def c2_copy(to, slot):
        return send(comb.at[to], landed.at[slot], c2_s.at[to], c2_r.at[slot], (z, 2 * to + c))

    def chunk_of(s):
        return (q // group + 1 + s) % CHUNKS

    def multiply(s):
        x = chunk_of(s)
        size = high // CHUNKS
        at = pl.multiple_of(x * size, size)
        th, tl = t_hi[pl.ds(at, size), :], t_lo[pl.ds(at, size), :]
        total = dot(th, w_hi[...]) + dot(tl, w_hi[...]) + dot(th, w_lo[...])
        tot[pl.ds(x * group, group)] = total.reshape(group, 2, per, rank)
        each(group, lambda i: c1_copy(x * group + i).start())

    def merge(s):
        x = chunk_of(s)

        def one(i):
            chip = x * group + i
            c1_copy(chip).wait_recv()
            value = tot[chip, c] + sib[chip]

            @pl.when(chip != q)
            def _():
                comb[chip] = value
                c2_copy(chip, q).start()

            @pl.when(chip == q)
            def _():
                landed[q] = value

        each(group, one)

    multiply(0)
    gram_3(0)

    def go(s):
        multiply(s + 1)
        merge(s)

    each(CHUNKS - 1, go)
    merge(CHUNKS - 1)

    gram_4(0)

    each(nq - 1, lambda s: c2_copy(q, (q + 1 + s) % nq).wait_recv())
    moments = landed[0]
    for s in range(1, nq):
        moments = moments + landed[s]
    rows_a = -full_dot(moments, system[...])
    fa_ref[...] = rows_a
    a_all[p] = rows_a

    def e1_copy(to, slot):
        return send(fa_ref, a_all.at[slot], e1_s.at[to], e_r.at[slot], (z, to))

    def e2_copy(slot):
        return send(a_all.at[slot], a_all.at[slot], e2_s.at[slot], e_r.at[slot], (z, other))

    gram_local(1, rows_a)
    gram_1(1)
    e1_copy(other, p).start()
    each(nq - 1, lambda s: e1_copy(2 * ((q + 1 + s) % nq) + c, p).start())
    gram_2(1)

    def forward(s):
        slot = 2 * ((q + nq - 1 - s) % nq) + c
        e1_copy(p, slot).wait_recv()
        e2_copy(slot).start()

    each(nq - 1, forward)
    gram_3(1)
    each(nq, lambda s: e2_copy(2 * ((q + nq - s) % nq) + 1 - c).wait_recv())

    piece = min(256, high)

    def turn(s):
        at = pl.multiple_of(s * piece, piece)
        block = a_all[pl.ds(s * (piece // per), piece // per)].reshape(piece, rank)
        hi, lo = split2(block.T)
        at_hi[:, pl.ds(at, piece)] = hi
        at_lo[:, pl.ds(at, piece)] = lo

    each(high // piece, turn)

    total_b = jnp.zeros((rank, wide), F32)
    for k in range(layers):
        th, tl = t_hi[:, k * wide : (k + 1) * wide], t_lo[:, k * wide : (k + 1) * wide]
        value = dot(at_hi[...], th) + dot(at_lo[...], th) + dot(at_hi[...], tl)
        total_b = total_b + value * c_turn[:, k : k + 1]
    tot_b[...] = total_b.T.reshape(nz, per, rank)

    def h_copy(to, slot):
        return send(tot_b.at[to], h_land.at[slot], h_s.at[to], h_r.at[slot], (to, p))

    each(nz - 1, lambda s: h_copy((z + 1 + s) % nz, z).start())
    h_land[z] = tot_b[z]

    gram_4(1)

    each(nz - 1, lambda s: h_copy(z, (z + 1 + s) % nz).wait_recv())
    moments = h_land[0]
    for s in range(1, nz):
        moments = moments + h_land[s]
    fb_ref[...] = -full_dot(moments, system[...])

    each(nz - 1, lambda s: a_copy((z + 1 + s) % nz, z).wait_send())
    each(nz - 1, lambda s: h_copy((z + 1 + s) % nz, z).wait_send())
    for t in range(2):
        each(nj - 1, lambda s: g1_copy(t, (p + 1 + s) % nj, p).wait_send())
        each(nz - 1, lambda s: g2_copy(t, (z + 1 + s) % nz, z).wait_send())
        each(nj - 1, lambda s: g3_copy(t, (p + 1 + s) % nj, p).wait_send())
    each(nq, lambda s: c1_copy(s).wait_send())
    each(nq - 1, lambda s: c2_copy((q + 1 + s) % nq, q).wait_send())
    e1_copy(other, p).wait_send()
    each(nq - 1, lambda s: e1_copy(2 * ((q + 1 + s) % nq) + c, p).wait_send())
    each(nq - 1, lambda s: e2_copy(2 * ((q + nq - 1 - s) % nq) + c).wait_send())


def solution(mesh):
    nz, nj = mesh.shape["ia"], mesh.shape["ja"]
    nq = nj // 2

    def local(tensor, factor_b, factor_c):
        layers, high, wide = tensor.shape
        per, rank = factor_b.shape
        slab = rank // nj
        vm = pltpu.VMEM
        sem = lambda *shape: pltpu.SemaphoreType.DMA(shape)
        out = jax.ShapeDtypeStruct((per, rank), F32)
        whole = pl.BlockSpec(memory_space=pltpu.VMEM)
        return pl.pallas_call(
            functools.partial(kernel, nz, nj),
            out_shape=(out, out),
            in_specs=[pl.BlockSpec(memory_space=pl.ANY), whole, whole],
            out_specs=(whole, whole),
            scratch_shapes=[
                vm((layers, high, wide), F32),
                vm((high, layers * wide), BF16), vm((high, layers * wide), BF16),
                vm((layers * wide, rank), BF16), vm((layers * wide, rank), BF16),
                vm((nz, per, rank), F32),
                vm((128, rank), F32), vm((rank, 128), F32), vm((rank, rank), F32),
                vm((2, nj, slab, rank), F32), vm((2, nj, slab, rank), F32), vm((2, slab, rank), F32),
                vm((2, nz, slab, rank), F32), vm((2, slab, rank), F32), vm((2, nj, slab, rank), F32),
                vm((rank, rank), F32),
                vm((nq, 2, per, rank), F32), vm((nq, per, rank), F32), vm((nq, per, rank), F32),
                vm((nq, per, rank), F32), vm((nj, per, rank), F32),
                vm((rank, high), BF16), vm((rank, high), BF16),
                vm((nz, per, rank), F32), vm((nz, per, rank), F32),
                sem(layers), sem(nz), sem(nz), sem(2, nj), sem(2, nj), sem(2, nz), sem(2, nz), sem(2, nj), sem(2, nj),
                sem(nq), sem(nq), sem(nq), sem(nq), sem(nj), sem(nj), sem(nj), sem(nz), sem(nz),
            ],
            compiler_params=pltpu.CompilerParams(
                collective_id=0, has_side_effects=True, vmem_limit_bytes=48 * 1024 * 1024
            ),
            cost_estimate=pl.CostEstimate(
                flops=4 * layers * high * wide * rank, bytes_accessed=4 * layers * high * wide, transcendentals=0
            ),
        )(tensor, factor_b, factor_c)

    in_specs = (P(None, "ia", "ja"), P(("ja", "ia"), None), P())
    out_specs = (P(("ia", "ja"), None), P(("ja", "ia"), None))
    return jax.shard_map(local, mesh=mesh, in_specs=in_specs, out_specs=out_specs, check_vma=False)
```

```python
import functools

import jax
import jax.numpy as jnp
from jax import lax
from jax.experimental import pallas as pl
from jax.experimental.pallas import tpu as pltpu
from jax.sharding import PartitionSpec as P

RIDGE = 0.001
MESH = pl.DeviceIdType.MESH
F32 = jnp.float32
BF16 = jnp.bfloat16
PB = 16
CHUNKS = 4
EARLY = 4


def split2(x):
    high = x.astype(BF16)
    return high, (x - high.astype(F32)).astype(BF16)


def split3(x):
    high = x.astype(BF16)
    rest = x - high.astype(F32)
    mid = rest.astype(BF16)
    return high, mid, (rest - mid.astype(F32)).astype(BF16)


def cross(left, right):
    lh, lm, ll = split3(left)
    rh, rm, rl = split3(right)
    a = jnp.concatenate([lh, lh, lm, lh, lm, ll], axis=0)
    b = jnp.concatenate([rh, rm, rh, rl, rm, rh], axis=0)
    return lax.dot_general(a, b, (((0,), (0,)), ((), ())), preferred_element_type=F32)


def row_of(block, at):
    return jnp.broadcast_to(block[at : at + 1, :], block.shape)


def eliminate(cols, panel, width):
    row = lax.broadcasted_iota(jnp.int32, (8, width), 0)
    halves = range(PB // 8)
    for j in range(0, PB, 2):
        h, jj = j // 8, j % 8
        u0, u1 = cols[j], cols[j + 1]
        first, second = row == jj, row == jj + 1
        pair = first | second
        a, b, d = row_of(u0[h], jj), row_of(u0[h], jj + 1), row_of(u1[h], jj + 1)
        scale = 1.0 / (a * d - b * b)
        w0 = [d * u0[g] - b * u1[g] for g in halves]
        w1 = [a * u1[g] - b * u0[g] for g in halves]
        w0[h] = jnp.where(first, -d, jnp.where(second, b, w0[h]))
        w1[h] = jnp.where(first, b, jnp.where(second, -a, w1[h]))

        def step(target):
            q0, q1 = row_of(target[h], jj), row_of(target[h], jj + 1)
            base = [jnp.where(pair, 0.0, target[g]) if g == h else target[g] for g in halves]
            return [base[g] - scale * (w0[g] * q0 + w1[g] * q1) for g in halves]

        cols = [step(col) if l > j + 1 else None for l, col in enumerate(cols)]
        panel = [step(part) for part in panel]
    return panel


def columns_of(panel, at, width):
    lanes = lax.broadcasted_iota(jnp.int32, panel.shape, 1)
    cols = []
    for l in range(PB):
        col = jnp.sum(jnp.where(lanes == at + l, panel, 0.0), axis=1, keepdims=True)
        col = jnp.broadcast_to(col, (PB, width))
        cols.append([col[8 * g : 8 * g + 8] for g in range(PB // 8)])
    return cols


def sweep(s_ref, between=()):
    size = s_ref.shape[0]
    steps = size // PB
    lanes = lax.broadcasted_iota(jnp.int32, (PB, size), 1)
    rows = lax.broadcasted_iota(jnp.int32, (PB, size), 0)
    whole = lax.broadcasted_iota(jnp.int32, (size, size), 1)
    width = 128

    def update(at, source, fresh):
        kept = jnp.where((whole >= at) & (whole < at + PB), 0.0, s_ref[...])
        s_ref[...] = kept - cross(source, fresh)

    def step(k, carry):
        panel, before, done = carry
        at = pl.multiple_of(k * PB, PB)
        after = pl.multiple_of(((k + 1) % steps) * PB, PB)
        cols = columns_of(panel, at, width)
        inside = (lanes >= at) & (lanes < at + PB)
        source = jnp.where(inside, jnp.where(lanes == at + rows, -1.0, 0.0), panel)
        parts = [
            [source[8 * g : 8 * g + 8, w * width : (w + 1) * width] for g in range(PB // 8)]
            for w in range(size // width)
        ]
        update(at - PB, before, done)
        following = s_ref[pl.ds(after, PB), :]
        factors = columns_of(following, at, width)
        parts = eliminate(cols, parts, width)
        fresh = jnp.concatenate([jnp.concatenate(part, axis=0) for part in parts], axis=1)
        s_ref[pl.ds(at, PB), :] = jnp.zeros((PB, size), F32)
        following = jnp.where(inside, 0.0, following)
        parts = [
            [following[8 * g : 8 * g + 8, w * width : (w + 1) * width] for g in range(PB // 8)]
            for w in range(size // width)
        ]
        for w in range(size // width):
            for l in range(PB):
                line = jnp.broadcast_to(fresh[l : l + 1, w * width : (w + 1) * width], (8, width))
                for g in range(PB // 8):
                    parts[w][g] = parts[w][g] - factors[l][g] * line
        following = jnp.concatenate([jnp.concatenate(part, axis=0) for part in parts], axis=1)
        return following, source, fresh

    blank = jnp.zeros((PB, size), F32)
    carry = (s_ref[0:PB, :], blank, blank)
    start = 0
    for end, action in between:
        carry = lax.fori_loop(start, end, step, carry)
        action()
        start = end
    _, before, done = lax.fori_loop(start, steps, step, carry)
    update(size - PB, before, done)


def dot(a, b):
    return jnp.dot(a, b, preferred_element_type=F32)


def full_dot(a, b):
    return jnp.dot(a, b, precision=lax.Precision.HIGHEST, preferred_element_type=F32)


def kernel(nz, nj, t_hbm, b_hbm, c_hbm, fa_ref, fb_ref,
           t_f32, t_hi, t_lo, w_hi, w_lo, b_all, b_sib, c_v, c_pad, c_turn, gram_c,
           gram, g1, g1_sum, g2, g2_sum, g3, inverse, system,
           tot, sib, comb, landed, own, m_all, total_b, tot_b, h_land,
           t_sem, in_sem, a_s, a_r, s_s, s_r, g1_s, g1_r, g2_s, g2_r, g3_s, g3_r, g4_s, g4_r,
           c1_s, c1_r, c2_s, c2_r, e1_s, e1_r, e2_s, e2_r, h_s, h_r):
    z, p = lax.axis_index("ia"), lax.axis_index("ja")
    q, c = p // 2, p % 2
    nq = nj // 2
    per, rank = own.shape
    layers, high, wide = t_hbm.shape
    half = rank // 2
    other = p + 1 - 2 * c

    def send(src, dst, s_sem, r_sem, to):
        return pltpu.make_async_remote_copy(
            src_ref=src, dst_ref=dst, send_sem=s_sem, recv_sem=r_sem, device_id=to, device_id_type=MESH
        )

    def arrived(ref, sem):
        pltpu.make_async_copy(ref, ref, sem).wait()

    def each(n, body):
        lax.fori_loop(0, n, lambda s, carry: (body(s), carry)[1], 0)

    def round_z(body):
        each(nz - 1, lambda s: body((z + 1 + (s + nz // 2 - 1) % (nz - 1)) % nz))

    def round_half(n, body):
        each(nz // 2 - 1, lambda s: body(n * (nz // 2) + (z + 1 + s) % (nz // 2)))

    def round_q(body):
        far = (nq // 2 + nq // 8 - 1) % (nq - 1)
        each(nq - 1, lambda s: body((q + 1 + (s + far) % (nq - 1)) % nq))

    barrier = pltpu.get_barrier_semaphore()
    round_q(lambda to: pl.semaphore_signal(barrier, inc=1, device_id=(z, 2 * to + c), device_id_type=MESH))
    round_z(lambda to: pl.semaphore_signal(barrier, inc=1, device_id=(to, p), device_id_type=MESH))
    pl.semaphore_signal(barrier, inc=1, device_id=(z, other), device_id_type=MESH)

    b_copy = pltpu.make_async_copy(b_hbm, b_all.at[z], in_sem.at[0])
    c_copy = pltpu.make_async_copy(c_hbm, c_v, in_sem.at[1])
    b_copy.start()
    c_copy.start()
    t_copies = [pltpu.make_async_copy(t_hbm.at[k], t_f32.at[k], t_sem.at[k]) for k in range(layers)]
    for copy in t_copies:
        copy.start()

    def g1_copy(t, to, slot):
        return send(gram.at[t, to], g1.at[t, slot], g1_s.at[t], g1_r.at[t], (z, 2 * to + c))

    def g2_copy(t, to, slot):
        return send(g1_sum.at[t], g2.at[t, slot], g2_s.at[t], g2_r.at[t], (to, p))

    def g3_copy(t, to, slot):
        return send(g2_sum.at[t], g3.at[t, c, slot], g3_s.at[t], g3_r.at[t], (z, 2 * to + c))

    def g4_copy(t, side):
        return send(g3.at[t, side], g3.at[t, side], g4_s.at[t], g4_r.at[t], (z, other))

    def gram_1(t, mine, twin):
        at = pl.multiple_of(c * half, half)
        left = jnp.concatenate([mine[:, pl.ds(at, half)], twin[:, pl.ds(at, half)]], axis=0)
        right = jnp.concatenate([mine[...], twin[...]], axis=0)
        value = cross(left, right).reshape(nq, half // nq, rank)
        gram[t] = value
        round_q(lambda to: g1_copy(t, to, q).start())
        g1[t, q] = gram[t, q]

    def gram_2(t):
        arrived(g1.at[t, pl.ds(0, nq - 1)], g1_r.at[t])
        total = g1[t, 0]
        for s in range(1, nq):
            total = total + g1[t, s]
        g1_sum[t] = total
        round_z(lambda to: g2_copy(t, to, z).start())
        g2[t, z] = total

    def gram_3(t):
        arrived(g2.at[t, pl.ds(0, nz - 1)], g2_r.at[t])
        total = g2[t, 0]
        for s in range(1, nz):
            total = total + g2[t, s]
        g2_sum[t] = total
        round_q(lambda to: g3_copy(t, to, q).start())
        g3[t, c, q] = total

    def gram_4(t):
        arrived(g3.at[t, 0, pl.ds(0, nq - 1)], g3_r.at[t])
        g4_copy(t, c).start()

    def gram_5(t):
        g4_copy(t, 1 - c).wait_recv()
        return g3[t].reshape(rank, rank)

    def system_of(value):
        rows = lax.broadcasted_iota(jnp.int32, (rank, rank), 0)
        lanes = lax.broadcasted_iota(jnp.int32, (rank, rank), 1)
        return gram_c[...] * value + jnp.where(rows == lanes, RIDGE, 0.0)

    def s_copy():
        return send(b_all.at[z], b_sib, s_s.at[0], s_r.at[0], (z, other))

    def a_copy(to, slot, which):
        return send(b_all.at[z], b_all.at[slot], a_s.at[0], a_r.at[which], (to, p))

    b_copy.wait()
    c_copy.wait()
    pl.semaphore_wait(barrier, nq - 1 + nz - 1 + 1)
    s_copy().start()
    round_half(z // (nz // 2), lambda to: a_copy(to, z, 0).start())
    each(nz // 2, lambda s: a_copy((1 - z // (nz // 2)) * (nz // 2) + (z + s) % (nz // 2), z, 1).start())
    s_copy().wait_recv()
    gram_1(0, b_all.at[z], b_sib)

    c_pad[...] = jnp.zeros_like(c_pad)
    c_pad[0:layers, :] = c_v[...]
    gram_c[...] = cross(c_pad[0:16, :], c_pad[0:16, :])
    c_turn[...] = c_pad[...].T

    hw = wide // 2
    sw = layers * hw
    strip = min(256, high)
    for k in range(layers):
        t_copies[k].wait()

        def convert(s, k=k):
            at = pl.multiple_of(s * strip, strip)
            hi, lo = split2(t_f32[k, pl.ds(at, strip), :])
            for n in range(2):
                to = n * sw + k * hw
                t_hi[pl.ds(at, strip), to : to + hw] = hi[:, n * hw : (n + 1) * hw]
                t_lo[pl.ds(at, strip), to : to + hw] = lo[:, n * hw : (n + 1) * hw]

        each(high // strip, convert)

    near = z // (nz // 2)

    def weights(n):
        block = b_all[pl.ds(n * (nz // 2), nz // 2)].reshape(hw, rank)
        for k in range(layers):
            hi, lo = split2(block * c_v[k : k + 1, :])
            at = pl.multiple_of(n * sw + k * hw, hw)
            w_hi[pl.ds(at, hw), :] = hi
            w_lo[pl.ds(at, hw), :] = lo

    def product(n, x):
        size = high // CHUNKS
        at, to = pl.multiple_of(x * size, size), pl.multiple_of(n * sw, sw)
        th, tl = t_hi[pl.ds(at, size), pl.ds(to, sw)], t_lo[pl.ds(at, size), pl.ds(to, sw)]
        wh, wl = w_hi[pl.ds(to, sw), :], w_lo[pl.ds(to, sw), :]
        return (dot(th, wh) + dot(tl, wh) + dot(th, wl)).reshape(nq // CHUNKS, 2, per, rank)

    if nz // 2 > 1:
        arrived(b_all.at[pl.ds(0, nz // 2 - 1)], a_r.at[0])
    weights(near)

    def first(x):
        tot[pl.ds(x * (nq // CHUNKS), nq // CHUNKS)] = product(near, x)

    each(CHUNKS, first)
    gram_2(0)
    arrived(b_all.at[pl.ds(0, nz // 2)], a_r.at[1])
    weights(1 - near)

    group = nq // CHUNKS

    def c1_copy(chip):
        return send(tot.at[chip, 1 - c], sib.at[chip], c1_s.at[0], c1_r.at[chip // group], (z, other))

    def c2_copy(to, slot):
        return send(comb.at[to], landed.at[slot], c2_s.at[0], c2_r.at[0], (z, 2 * to + c))

    def chunk_of(s):
        return (q // group + 1 + s) % CHUNKS

    def multiply(s):
        x = chunk_of(s)
        tot[pl.ds(x * group, group)] += product(1 - near, x)
        each(group, lambda i: c1_copy(x * group + i).start())

    def merge(s):
        x = chunk_of(s)

        arrived(sib.at[pl.ds(0, group)], c1_r.at[x])

        def one(i):
            chip = x * group + i
            value = tot[chip, c] + sib[chip]

            @pl.when(chip != q)
            def _():
                comb[chip] = value
                c2_copy(chip, q).start()

            @pl.when(chip == q)
            def _():
                landed[q] = value

        each(group, one)

    multiply(0)

    def go(s):
        multiply(s + 1)
        merge(s)

    each(CHUNKS - 1, go)
    merge(CHUNKS - 1)
    gram_3(0)

    def e1_copy(to):
        return send(own, m_all.at[p], e1_s.at[0], e1_r.at[q // group], (z, to))

    def twin_copy():
        return send(own, m_all.at[p], e1_s.at[1], e1_r.at[CHUNKS], (z, other))

    def e2_copy(slot, x):
        return send(m_all.at[slot], m_all.at[slot], e2_s.at[0], e2_r.at[x], (z, other))

    def moments_a():
        arrived(landed.at[pl.ds(0, nq - 1)], c2_r.at[0])
        moments = landed[0]
        for s in range(1, nq):
            moments = moments + landed[s]
        own[...] = moments
        twin_copy().start()
        m_all[p] = moments

    def share_moments():
        twin_copy().wait_recv()
        gram_1(1, own, m_all.at[other])
        round_q(lambda to: e1_copy(2 * to + c).start())

    gram_4(0)
    inverse[...] = system_of(gram_5(0))
    sweep(inverse, ((EARLY, moments_a), (EARLY + 2, share_moments)))
    fa_ref[...] = -full_dot(own[...], inverse[...])

    def group_of(s):
        return (q // group + s + s // 2 - 2 * (s // 3)) % CHUNKS

    def landing(s, sem):
        @pl.when(s == 0)
        def _():
            if group > 1:
                arrived(m_all.at[pl.ds(0, group - 1)], sem)

        @pl.when(s != 0)
        def _():
            arrived(m_all.at[pl.ds(0, group)], sem)

    def forward(s):
        x = group_of(s)
        landing(s, e1_r.at[x])

        def one(i):
            chip = x * group + i

            @pl.when(chip != q)
            def _():
                e2_copy(2 * chip + c, x).start()

        each(group, one)

    def back(s):
        x = group_of(s)
        landing(s, e2_r.at[x])
        size = high // CHUNKS
        at = pl.multiple_of(x * size, size)
        block = m_all[pl.ds(x * 2 * group, 2 * group)].reshape(size, rank)
        ah, al = split2(-full_dot(block, inverse[...]).T)
        for n in range(2):
            part = total_b[n]
            for m in range(layers // 2):
                to = n * sw + m * wide
                th, tl = t_hi[pl.ds(at, size), to : to + wide], t_lo[pl.ds(at, size), to : to + wide]
                value = dot(ah, th) + dot(al, th) + dot(ah, tl)
                part = part + value[:, 0:hw] * c_turn[:, 2 * m : 2 * m + 1]
                part = part + value[:, hw:wide] * c_turn[:, 2 * m + 1 : 2 * m + 2]
            total_b[n] = part

    total_b[...] = jnp.zeros_like(total_b)
    forward(0)
    gram_2(1)

    def go_back(s):
        forward(s + 1)
        back(s)

        @pl.when(s == 1)
        def _():
            gram_3(1)

    each(CHUNKS - 1, go_back)
    back(CHUNKS - 1)

    for n in range(2):
        tot_b[n * (nz // 2) : (n + 1) * (nz // 2)] = total_b[n].T.reshape(nz // 2, per, rank)

    def h_copy(to, slot):
        return send(tot_b.at[to], h_land.at[slot], h_s.at[0], h_r.at[0], (to, p))

    round_z(lambda to: h_copy(to, z).start())
    gram_4(1)
    h_land[z] = tot_b[z]

    system[...] = full_dot(inverse[...], gram_5(1))
    system[...] = system_of(full_dot(system[...], inverse[...]))
    sweep(system)

    arrived(h_land.at[pl.ds(0, nz - 1)], h_r.at[0])
    moments = h_land[0]
    for s in range(1, nz):
        moments = moments + h_land[s]
    fb_ref[...] = -full_dot(moments, system[...])

    s_copy().wait_send()
    arrived(b_all.at[pl.ds(0, nz - 1)], a_s.at[0])
    arrived(h_land.at[pl.ds(0, nz - 1)], h_s.at[0])
    for t in range(2):
        arrived(g1.at[t, pl.ds(0, nq - 1)], g1_s.at[t])
        arrived(g2.at[t, pl.ds(0, nz - 1)], g2_s.at[t])
        arrived(g3.at[t, 0, pl.ds(0, nq - 1)], g3_s.at[t])
        g4_copy(t, c).wait_send()
    arrived(sib, c1_s.at[0])
    arrived(landed.at[pl.ds(0, nq - 1)], c2_s.at[0])
    arrived(m_all.at[pl.ds(0, nq - 1)], e1_s.at[0])
    twin_copy().wait_send()
    arrived(m_all.at[pl.ds(0, nq - 1)], e2_s.at[0])


def solution(mesh):
    nz, nj = mesh.shape["ia"], mesh.shape["ja"]
    nq = nj // 2

    def local(tensor, factor_b, factor_c):
        layers, high, wide = tensor.shape
        per, rank = factor_b.shape
        slab = rank // nj
        vm = pltpu.VMEM
        sem = lambda *shape: pltpu.SemaphoreType.DMA(shape)
        out = jax.ShapeDtypeStruct((per, rank), F32)
        whole = pl.BlockSpec(memory_space=pltpu.VMEM)
        anywhere = pl.BlockSpec(memory_space=pltpu.HBM)
        return pl.pallas_call(
            functools.partial(kernel, nz, nj),
            out_shape=(out, out),
            in_specs=[anywhere] * 3,
            out_specs=(whole, whole),
            scratch_shapes=[
                vm((layers, high, wide), F32),
                vm((high, layers * wide), BF16), vm((high, layers * wide), BF16),
                vm((layers * wide, rank), BF16), vm((layers * wide, rank), BF16),
                vm((nz, per, rank), F32), vm((per, rank), F32), vm((layers, rank), F32),
                vm((128, rank), F32), vm((rank, 128), F32), vm((rank, rank), F32),
                vm((2, nq, slab, rank), F32), vm((2, nq, slab, rank), F32), vm((2, slab, rank), F32),
                vm((2, nz, slab, rank), F32), vm((2, slab, rank), F32), vm((2, 2, nq, slab, rank), F32),
                vm((rank, rank), F32), vm((rank, rank), F32),
                vm((nq, 2, per, rank), F32), vm((nq, per, rank), F32), vm((nq, per, rank), F32),
                vm((nq, per, rank), F32), vm((per, rank), F32), vm((nj, per, rank), F32),
                vm((2, rank, wide // 2), F32),
                vm((nz, per, rank), F32), vm((nz, per, rank), F32),
                sem(layers), sem(2), sem(1), sem(2), sem(1), sem(1),
                sem(2), sem(2), sem(2), sem(2), sem(2), sem(2), sem(2), sem(2),
                sem(1), sem(CHUNKS), sem(1), sem(1), sem(2), sem(CHUNKS + 1), sem(1), sem(CHUNKS), sem(1), sem(1),
            ],
            compiler_params=pltpu.CompilerParams(
                collective_id=0, has_side_effects=True, vmem_limit_bytes=48 * 1024 * 1024
            ),
            cost_estimate=pl.CostEstimate(
                flops=4 * layers * high * wide * rank, bytes_accessed=4 * layers * high * wide, transcendentals=0
            ),
        )(tensor, factor_b, factor_c)

    in_specs = (P(None, "ia", "ja"), P(("ja", "ia"), None), P())
    out_specs = (P(("ia", "ja"), None), P(("ja", "ia"), None))
    return jax.shard_map(local, mesh=mesh, in_specs=in_specs, out_specs=out_specs, check_vma=False)
```

```python
import functools

import jax
import jax.numpy as jnp
from jax import lax
from jax.experimental import pallas as pl
from jax.experimental.pallas import tpu as pltpu
from jax.sharding import PartitionSpec as P

RIDGE = 0.001
MESH = pl.DeviceIdType.MESH
F32 = jnp.float32
BF16 = jnp.bfloat16
PB = 16
CHUNKS = 4
MIDDLE = 5


def split2(x):
    high = x.astype(BF16)
    return high, (x - high.astype(F32)).astype(BF16)


def split3(x):
    high = x.astype(BF16)
    rest = x - high.astype(F32)
    mid = rest.astype(BF16)
    return high, mid, (rest - mid.astype(F32)).astype(BF16)


def cross(left, right):
    lh, lm, ll = split3(left)
    rh, rm, rl = split3(right)
    a = jnp.concatenate([lh, lh, lm, lh, lm, ll], axis=0)
    b = jnp.concatenate([rh, rm, rh, rl, rm, rh], axis=0)
    return lax.dot_general(a, b, (((0,), (0,)), ((), ())), preferred_element_type=F32)


def row_of(block, at):
    return jnp.broadcast_to(block[at : at + 1, :], block.shape)


def eliminate(cols, panel, width):
    row = lax.broadcasted_iota(jnp.int32, (8, width), 0)
    halves = range(PB // 8)
    for j in range(0, PB, 2):
        h, jj = j // 8, j % 8
        u0, u1 = cols[j], cols[j + 1]
        first, second = row == jj, row == jj + 1
        pair = first | second
        a, b, d = row_of(u0[h], jj), row_of(u0[h], jj + 1), row_of(u1[h], jj + 1)
        scale = 1.0 / (a * d - b * b)
        w0 = [d * u0[g] - b * u1[g] for g in halves]
        w1 = [a * u1[g] - b * u0[g] for g in halves]
        w0[h] = jnp.where(first, -d, jnp.where(second, b, w0[h]))
        w1[h] = jnp.where(first, b, jnp.where(second, -a, w1[h]))

        def step(target):
            q0, q1 = row_of(target[h], jj), row_of(target[h], jj + 1)
            base = [jnp.where(pair, 0.0, target[g]) if g == h else target[g] for g in halves]
            return [base[g] - scale * (w0[g] * q0 + w1[g] * q1) for g in halves]

        cols = [step(col) if l > j + 1 else None for l, col in enumerate(cols)]
        panel = [step(part) for part in panel]
    return panel


def columns_of(panel, at, width):
    lanes = lax.broadcasted_iota(jnp.int32, panel.shape, 1)
    cols = []
    for l in range(PB):
        col = jnp.sum(jnp.where(lanes == at + l, panel, 0.0), axis=1, keepdims=True)
        col = jnp.broadcast_to(col, (PB, width))
        cols.append([col[8 * g : 8 * g + 8] for g in range(PB // 8)])
    return cols


def parts_of(panel, width):
    return [
        [panel[8 * g : 8 * g + 8, w * width : (w + 1) * width] for g in range(PB // 8)]
        for w in range(panel.shape[1] // width)
    ]


def whole_of(parts):
    return jnp.concatenate([jnp.concatenate(part, axis=0) for part in parts], axis=1)


def less(panel, factors, fresh, width):
    parts = parts_of(panel, width)
    for l in range(PB):
        for w, part in enumerate(parts):
            line = jnp.broadcast_to(fresh[l : l + 1, w * width : (w + 1) * width], (8, width))
            for g in range(PB // 8):
                part[g] = part[g] - factors[l][g] * line
    return whole_of(parts)


def sweep(s_ref, between=()):
    size = s_ref.shape[0]
    steps = size // (2 * PB)
    lanes = lax.broadcasted_iota(jnp.int32, (PB, size), 1)
    rows = lax.broadcasted_iota(jnp.int32, (PB, size), 0)
    whole = lax.broadcasted_iota(jnp.int32, (size, size), 1)
    width = 128

    def step(k, carry):
        at = pl.multiple_of(k * 2 * PB, 2 * PB)
        mid = at + PB
        upper, lower = s_ref[pl.ds(at, PB), :], s_ref[pl.ds(pl.multiple_of(mid, PB), PB), :]
        in_upper, in_lower = (lanes >= at) & (lanes < mid), (lanes >= mid) & (lanes < mid + PB)
        minus_upper = jnp.where(lanes == at + rows, -1.0, 0.0)
        minus_lower = jnp.where(lanes == mid + rows, -1.0, 0.0)
        cols = columns_of(upper, at, width)
        factors = columns_of(lower, at, width)
        first = whole_of(eliminate(cols, parts_of(jnp.where(in_upper, minus_upper, upper), width), width))
        backs = columns_of(first, mid, width)
        rest = less(jnp.where(in_upper, 0.0, lower), factors, first, width)
        cols = columns_of(rest, mid, width)
        second = whole_of(eliminate(cols, parts_of(jnp.where(in_lower, minus_lower, rest), width), width))
        first = less(jnp.where(in_lower, 0.0, first), backs, second, width)
        fresh = jnp.concatenate([first, second], axis=0)
        both = in_upper | in_lower
        source = jnp.concatenate([jnp.where(both, minus_upper, upper), jnp.where(both, minus_lower, lower)], axis=0)
        kept = jnp.where((whole >= at) & (whole < at + 2 * PB), 0.0, s_ref[...])
        s_ref[...] = kept - cross(source, fresh)
        s_ref[pl.ds(at, 2 * PB), :] = fresh
        return carry

    start = 0
    for end, action in between:
        lax.fori_loop(start, end, step, 0)
        action()
        start = end
    lax.fori_loop(start, steps, step, 0)


def dot(a, b):
    return jnp.dot(a, b, preferred_element_type=F32)


def full_dot(a, b):
    return jnp.dot(a, b, precision=lax.Precision.HIGHEST, preferred_element_type=F32)


def kernel(nz, nj, t_hbm, b_hbm, c_hbm, fa_ref, fb_ref,
           t_f32, t_hi, t_lo, w_hi, w_lo, b_all, b_sib, c_v, c_pad, c_turn, gram_c,
           gram, g1, g1_sum, g2, g2_sum, g3, inverse, system,
           tot, sib, comb, landed, own, m_all, total_b, tot_b, h_land,
           t_sem, in_sem, a_s, a_r, s_s, s_r, g1_s, g1_r, g2_s, g2_r, g3_s, g3_r, g4_s, g4_r,
           c1_s, c1_r, c2_s, c2_r, e1_s, e1_r, e2_s, e2_r, h_s, h_r):
    z, p = lax.axis_index("ia"), lax.axis_index("ja")
    q, c = p // 2, p % 2
    nq = nj // 2
    per, rank = own.shape
    layers, high, wide = t_hbm.shape
    half = rank // 2
    other = p + 1 - 2 * c

    def send(src, dst, s_sem, r_sem, to):
        return pltpu.make_async_remote_copy(
            src_ref=src, dst_ref=dst, send_sem=s_sem, recv_sem=r_sem, device_id=to, device_id_type=MESH
        )

    def arrived(ref, sem):
        pltpu.make_async_copy(ref, ref, sem).wait()

    def each(n, body):
        lax.fori_loop(0, n, lambda s, carry: (body(s), carry)[1], 0)

    def round_z(body):
        each(nz - 1, lambda s: body((z + 1 + (s + nz // 2 - 1) % (nz - 1)) % nz))

    def round_half(n, body):
        each(nz // 2 - 1, lambda s: body(n * (nz // 2) + (z + 1 + s) % (nz // 2)))

    def round_q(body):
        far = (nq // 2 + nq // 8 - 1) % (nq - 1)
        each(nq - 1, lambda s: body((q + 1 + (s + far) % (nq - 1)) % nq))

    barrier = pltpu.get_barrier_semaphore()
    round_q(lambda to: pl.semaphore_signal(barrier, inc=1, device_id=(z, 2 * to + c), device_id_type=MESH))
    round_z(lambda to: pl.semaphore_signal(barrier, inc=1, device_id=(to, p), device_id_type=MESH))
    pl.semaphore_signal(barrier, inc=1, device_id=(z, other), device_id_type=MESH)

    b_copy = pltpu.make_async_copy(b_hbm, b_all.at[z], in_sem.at[0])
    c_copy = pltpu.make_async_copy(c_hbm, c_v, in_sem.at[1])
    b_copy.start()
    c_copy.start()
    t_copies = [pltpu.make_async_copy(t_hbm.at[k], t_f32.at[k], t_sem.at[k]) for k in range(layers)]
    for copy in t_copies:
        copy.start()

    def g1_copy(t, to, slot):
        return send(gram.at[t, to], g1.at[t, slot], g1_s.at[t], g1_r.at[t], (z, 2 * to + c))

    def g2_copy(t, to, slot):
        return send(g1_sum.at[t], g2.at[t, slot], g2_s.at[t], g2_r.at[t], (to, p))

    def g3_copy(t, to, slot):
        return send(g2_sum.at[t], g3.at[t, c, slot], g3_s.at[t], g3_r.at[t], (z, 2 * to + c))

    def g4_copy(t, side):
        return send(g3.at[t, side], g3.at[t, side], g4_s.at[t], g4_r.at[t], (z, other))

    def gram_1(t, mine, twin):
        at = pl.multiple_of(c * half, half)
        left = jnp.concatenate([mine[:, pl.ds(at, half)], twin[:, pl.ds(at, half)]], axis=0)
        right = jnp.concatenate([mine[...], twin[...]], axis=0)
        value = cross(left, right).reshape(nq, half // nq, rank)
        gram[t] = value
        round_q(lambda to: g1_copy(t, to, q).start())
        g1[t, q] = gram[t, q]

    def gram_2(t):
        arrived(g1.at[t, pl.ds(0, nq - 1)], g1_r.at[t])
        total = g1[t, 0]
        for s in range(1, nq):
            total = total + g1[t, s]
        g1_sum[t] = total
        round_z(lambda to: g2_copy(t, to, z).start())
        g2[t, z] = total

    def gram_3(t):
        arrived(g2.at[t, pl.ds(0, nz - 1)], g2_r.at[t])
        total = g2[t, 0]
        for s in range(1, nz):
            total = total + g2[t, s]
        g2_sum[t] = total
        round_q(lambda to: g3_copy(t, to, q).start())
        g3[t, c, q] = total

    def gram_4(t):
        arrived(g3.at[t, 0, pl.ds(0, nq - 1)], g3_r.at[t])
        g4_copy(t, c).start()

    def gram_5(t):
        g4_copy(t, 1 - c).wait_recv()
        return g3[t].reshape(rank, rank)

    def system_of(value):
        rows = lax.broadcasted_iota(jnp.int32, (rank, rank), 0)
        lanes = lax.broadcasted_iota(jnp.int32, (rank, rank), 1)
        return gram_c[...] * value + jnp.where(rows == lanes, RIDGE, 0.0)

    def s_copy():
        return send(b_all.at[z], b_sib, s_s.at[0], s_r.at[0], (z, other))

    def a_copy(to, slot, which):
        return send(b_all.at[z], b_all.at[slot], a_s.at[0], a_r.at[which], (to, p))

    b_copy.wait()
    c_copy.wait()
    pl.semaphore_wait(barrier, nq - 1 + nz - 1 + 1)
    s_copy().start()
    round_half(z // (nz // 2), lambda to: a_copy(to, z, 0).start())
    each(nz // 2, lambda s: a_copy((1 - z // (nz // 2)) * (nz // 2) + (z + s) % (nz // 2), z, 1).start())
    s_copy().wait_recv()
    gram_1(0, b_all.at[z], b_sib)

    c_pad[...] = jnp.zeros_like(c_pad)
    c_pad[0:layers, :] = c_v[...]
    gram_c[...] = cross(c_pad[0:16, :], c_pad[0:16, :])
    c_turn[...] = c_pad[...].T

    hw = wide // 2
    sw = layers * hw
    strip = min(256, high)
    for k in range(layers):
        t_copies[k].wait()

        def convert(s, k=k):
            at = pl.multiple_of(s * strip, strip)
            hi, lo = split2(t_f32[k, pl.ds(at, strip), :])
            for n in range(2):
                to = n * sw + k * hw
                t_hi[pl.ds(at, strip), to : to + hw] = hi[:, n * hw : (n + 1) * hw]
                t_lo[pl.ds(at, strip), to : to + hw] = lo[:, n * hw : (n + 1) * hw]

        each(high // strip, convert)

    near = z // (nz // 2)

    def weights(n):
        block = b_all[pl.ds(n * (nz // 2), nz // 2)].reshape(hw, rank)
        for k in range(layers):
            hi, lo = split2(block * c_v[k : k + 1, :])
            at = pl.multiple_of(n * sw + k * hw, hw)
            w_hi[pl.ds(at, hw), :] = hi
            w_lo[pl.ds(at, hw), :] = lo

    def product(n, x):
        size = high // CHUNKS
        at, to = pl.multiple_of(x * size, size), pl.multiple_of(n * sw, sw)
        th, tl = t_hi[pl.ds(at, size), pl.ds(to, sw)], t_lo[pl.ds(at, size), pl.ds(to, sw)]
        wh, wl = w_hi[pl.ds(to, sw), :], w_lo[pl.ds(to, sw), :]
        return (dot(th, wh) + dot(tl, wh) + dot(th, wl)).reshape(nq // CHUNKS, 2, per, rank)

    if nz // 2 > 1:
        arrived(b_all.at[pl.ds(0, nz // 2 - 1)], a_r.at[0])
    weights(near)

    def first(x):
        tot[pl.ds(x * (nq // CHUNKS), nq // CHUNKS)] = product(near, x)

    each(CHUNKS, first)
    gram_2(0)
    arrived(b_all.at[pl.ds(0, nz // 2)], a_r.at[1])
    weights(1 - near)

    group = nq // CHUNKS

    def c1_copy(chip):
        return send(tot.at[chip, 1 - c], sib.at[chip], c1_s.at[0], c1_r.at[chip // group], (z, other))

    def c2_copy(to, slot):
        return send(comb.at[to], landed.at[slot], c2_s.at[0], c2_r.at[0], (z, 2 * to + c))

    def chunk_of(s):
        return (q // group + 1 + s) % CHUNKS

    def multiply(s):
        x = chunk_of(s)
        tot[pl.ds(x * group, group)] += product(1 - near, x)
        each(group, lambda i: c1_copy(x * group + i).start())

    def merge(s):
        x = chunk_of(s)

        arrived(sib.at[pl.ds(0, group)], c1_r.at[x])

        def one(i):
            chip = x * group + i
            value = tot[chip, c] + sib[chip]

            @pl.when(chip != q)
            def _():
                comb[chip] = value
                c2_copy(chip, q).start()

            @pl.when(chip == q)
            def _():
                landed[q] = value

        each(group, one)

    multiply(0)

    def go(s):
        multiply(s + 1)
        merge(s)

    each(CHUNKS - 1, go)
    gram_3(0)
    merge(CHUNKS - 1)

    def e1_copy(to):
        return send(own, m_all.at[p], e1_s.at[0], e1_r.at[q // group], (z, to))

    def twin_copy():
        return send(own, m_all.at[p], e1_s.at[1], e1_r.at[CHUNKS], (z, other))

    def e2_copy(slot, x):
        return send(m_all.at[slot], m_all.at[slot], e2_s.at[0], e2_r.at[x], (z, other))

    def moments_a():
        arrived(landed.at[pl.ds(0, nq - 1)], c2_r.at[0])
        moments = landed[0]
        for s in range(1, nq):
            moments = moments + landed[s]
        own[...] = moments
        twin_copy().start()
        m_all[p] = moments

    def share_moments():
        twin_copy().wait_recv()
        gram_1(1, own, m_all.at[other])
        round_q(lambda to: e1_copy(2 * to + c).start())

    moments_a()
    share_moments()
    gram_4(0)
    inverse[...] = system_of(gram_5(0))
    sweep(inverse, ((MIDDLE, lambda: gram_2(1)),))
    fa_ref[...] = -full_dot(own[...], inverse[...])

    def group_of(s):
        return (q // group + s + s // 2 - 2 * (s // 3)) % CHUNKS

    def landing(s, sem):
        @pl.when(s == 0)
        def _():
            if group > 1:
                arrived(m_all.at[pl.ds(0, group - 1)], sem)

        @pl.when(s != 0)
        def _():
            arrived(m_all.at[pl.ds(0, group)], sem)

    def forward(s):
        x = group_of(s)
        landing(s, e1_r.at[x])

        def one(i):
            chip = x * group + i

            @pl.when(chip != q)
            def _():
                e2_copy(2 * chip + c, x).start()

        each(group, one)

    def back(s):
        x = group_of(s)
        landing(s, e2_r.at[x])
        size = high // CHUNKS
        at = pl.multiple_of(x * size, size)
        block = m_all[pl.ds(x * 2 * group, 2 * group)].reshape(size, rank)
        mh, ml = split2(block)
        ih, il = split2(inverse[...])
        ah, al = split2(-(dot(mh, ih) + dot(ml, ih) + dot(mh, il)).T)
        for n in range(2):
            part = total_b[n]
            for m in range(layers // 2):
                to = n * sw + m * wide
                th, tl = t_hi[pl.ds(at, size), to : to + wide], t_lo[pl.ds(at, size), to : to + wide]
                value = dot(ah, th) + dot(al, th) + dot(ah, tl)
                part = part + value[:, 0:hw] * c_turn[:, 2 * m : 2 * m + 1]
                part = part + value[:, hw:wide] * c_turn[:, 2 * m + 1 : 2 * m + 2]
            total_b[n] = part

    total_b[...] = jnp.zeros_like(total_b)
    forward(0)

    def go_back(s):
        forward(s + 1)
        back(s)

        @pl.when(s == 0)
        def _():
            gram_3(1)

    each(CHUNKS - 1, go_back)
    back(CHUNKS - 1)

    for n in range(2):
        tot_b[n * (nz // 2) : (n + 1) * (nz // 2)] = total_b[n].T.reshape(nz // 2, per, rank)

    def h_copy(to, slot):
        return send(tot_b.at[to], h_land.at[slot], h_s.at[0], h_r.at[0], (to, p))

    round_z(lambda to: h_copy(to, z).start())
    gram_4(1)
    h_land[z] = tot_b[z]

    system[...] = full_dot(inverse[...], gram_5(1))
    system[...] = system_of(full_dot(system[...], inverse[...]))
    sweep(system)

    arrived(h_land.at[pl.ds(0, nz - 1)], h_r.at[0])
    moments = h_land[0]
    for s in range(1, nz):
        moments = moments + h_land[s]
    fb_ref[...] = -full_dot(moments, system[...])

    s_copy().wait_send()
    arrived(b_all.at[pl.ds(0, nz - 1)], a_s.at[0])
    arrived(h_land.at[pl.ds(0, nz - 1)], h_s.at[0])
    for t in range(2):
        arrived(g1.at[t, pl.ds(0, nq - 1)], g1_s.at[t])
        arrived(g2.at[t, pl.ds(0, nz - 1)], g2_s.at[t])
        arrived(g3.at[t, 0, pl.ds(0, nq - 1)], g3_s.at[t])
        g4_copy(t, c).wait_send()
    arrived(sib, c1_s.at[0])
    arrived(landed.at[pl.ds(0, nq - 1)], c2_s.at[0])
    arrived(m_all.at[pl.ds(0, nq - 1)], e1_s.at[0])
    twin_copy().wait_send()
    arrived(m_all.at[pl.ds(0, nq - 1)], e2_s.at[0])


def solution(mesh):
    nz, nj = mesh.shape["ia"], mesh.shape["ja"]
    nq = nj // 2

    def local(tensor, factor_b, factor_c):
        layers, high, wide = tensor.shape
        per, rank = factor_b.shape
        slab = rank // nj
        vm = pltpu.VMEM
        sem = lambda *shape: pltpu.SemaphoreType.DMA(shape)
        out = jax.ShapeDtypeStruct((per, rank), F32)
        whole = pl.BlockSpec(memory_space=pltpu.VMEM)
        anywhere = pl.BlockSpec(memory_space=pltpu.HBM)
        return pl.pallas_call(
            functools.partial(kernel, nz, nj),
            out_shape=(out, out),
            in_specs=[anywhere] * 3,
            out_specs=(whole, whole),
            scratch_shapes=[
                vm((layers, high, wide), F32),
                vm((high, layers * wide), BF16), vm((high, layers * wide), BF16),
                vm((layers * wide, rank), BF16), vm((layers * wide, rank), BF16),
                vm((nz, per, rank), F32), vm((per, rank), F32), vm((layers, rank), F32),
                vm((128, rank), F32), vm((rank, 128), F32), vm((rank, rank), F32),
                vm((2, nq, slab, rank), F32), vm((2, nq, slab, rank), F32), vm((2, slab, rank), F32),
                vm((2, nz, slab, rank), F32), vm((2, slab, rank), F32), vm((2, 2, nq, slab, rank), F32),
                vm((rank, rank), F32), vm((rank, rank), F32),
                vm((nq, 2, per, rank), F32), vm((nq, per, rank), F32), vm((nq, per, rank), F32),
                vm((nq, per, rank), F32), vm((per, rank), F32), vm((nj, per, rank), F32),
                vm((2, rank, wide // 2), F32),
                vm((nz, per, rank), F32), vm((nz, per, rank), F32),
                sem(layers), sem(2), sem(1), sem(2), sem(1), sem(1),
                sem(2), sem(2), sem(2), sem(2), sem(2), sem(2), sem(2), sem(2),
                sem(1), sem(CHUNKS), sem(1), sem(1), sem(2), sem(CHUNKS + 1), sem(1), sem(CHUNKS), sem(1), sem(1),
            ],
            compiler_params=pltpu.CompilerParams(
                collective_id=0, has_side_effects=True, vmem_limit_bytes=48 * 1024 * 1024
            ),
            cost_estimate=pl.CostEstimate(
                flops=4 * layers * high * wide * rank, bytes_accessed=4 * layers * high * wide, transcendentals=0
            ),
        )(tensor, factor_b, factor_c)

    in_specs = (P(None, "ia", "ja"), P(("ja", "ia"), None), P())
    out_specs = (P(("ia", "ja"), None), P(("ja", "ia"), None))
    return jax.shard_map(local, mesh=mesh, in_specs=in_specs, out_specs=out_specs, check_vma=False)
```

```python
import functools

import jax
import jax.numpy as jnp
from jax import lax
from jax.experimental import pallas as pl
from jax.experimental.pallas import tpu as pltpu
from jax.sharding import PartitionSpec as P

RIDGE = 0.001
MESH = pl.DeviceIdType.MESH
F32 = jnp.float32
BF16 = jnp.bfloat16
PB = 16
CHUNKS = 4
MIDDLE = 6


def split2(x):
    high = x.astype(BF16)
    return high, (x - high.astype(F32)).astype(BF16)


def split3(x):
    high = x.astype(BF16)
    rest = x - high.astype(F32)
    mid = rest.astype(BF16)
    return high, mid, (rest - mid.astype(F32)).astype(BF16)


def cross(left, right):
    lh, lm, ll = split3(left)
    rh, rm, rl = split3(right)
    a = jnp.concatenate([lh, lh, lm, lh, lm, ll], axis=0)
    b = jnp.concatenate([rh, rm, rh, rl, rm, rh], axis=0)
    return lax.dot_general(a, b, (((0,), (0,)), ((), ())), preferred_element_type=F32)


def row_of(block, at):
    return jnp.broadcast_to(block[at : at + 1, :], block.shape)


def eliminate(cols, panel, width):
    row = lax.broadcasted_iota(jnp.int32, (8, width), 0)
    halves = range(PB // 8)
    for j in range(0, PB, 2):
        h, jj = j // 8, j % 8
        u0, u1 = cols[j], cols[j + 1]
        first, second = row == jj, row == jj + 1
        pair = first | second
        a, b, d = row_of(u0[h], jj), row_of(u0[h], jj + 1), row_of(u1[h], jj + 1)
        scale = 1.0 / (a * d - b * b)
        w0 = [d * u0[g] - b * u1[g] for g in halves]
        w1 = [a * u1[g] - b * u0[g] for g in halves]
        w0[h] = jnp.where(first, -d, jnp.where(second, b, w0[h]))
        w1[h] = jnp.where(first, b, jnp.where(second, -a, w1[h]))

        def step(target):
            q0, q1 = row_of(target[h], jj), row_of(target[h], jj + 1)
            base = [jnp.where(pair, 0.0, target[g]) if g == h else target[g] for g in halves]
            return [base[g] - scale * (w0[g] * q0 + w1[g] * q1) for g in halves]

        cols = [step(col) if l > j + 1 else None for l, col in enumerate(cols)]
        panel = [step(part) for part in panel]
    return panel


def columns_of(panel, at, width):
    lanes = lax.broadcasted_iota(jnp.int32, panel.shape, 1)
    cols = []
    for l in range(PB):
        col = jnp.sum(jnp.where(lanes == at + l, panel, 0.0), axis=1, keepdims=True)
        col = jnp.broadcast_to(col, (PB, width))
        cols.append([col[8 * g : 8 * g + 8] for g in range(PB // 8)])
    return cols


def parts_of(panel, width):
    return [
        [panel[8 * g : 8 * g + 8, w * width : (w + 1) * width] for g in range(PB // 8)]
        for w in range(panel.shape[1] // width)
    ]


def whole_of(parts):
    return jnp.concatenate([jnp.concatenate(part, axis=0) for part in parts], axis=1)


def less(panel, factors, fresh, width):
    parts = parts_of(panel, width)
    for l in range(PB):
        for w, part in enumerate(parts):
            line = jnp.broadcast_to(fresh[l : l + 1, w * width : (w + 1) * width], (8, width))
            for g in range(PB // 8):
                part[g] = part[g] - factors[l][g] * line
    return whole_of(parts)


def sweep(s_ref, between=()):
    size = s_ref.shape[0]
    steps = size // (2 * PB)
    lanes = lax.broadcasted_iota(jnp.int32, (PB, size), 1)
    rows = lax.broadcasted_iota(jnp.int32, (PB, size), 0)
    whole = lax.broadcasted_iota(jnp.int32, (size, size), 1)
    width = 128

    def step(k, carry):
        at = pl.multiple_of(k * 2 * PB, 2 * PB)
        mid = at + PB
        upper, lower = s_ref[pl.ds(at, PB), :], s_ref[pl.ds(pl.multiple_of(mid, PB), PB), :]
        in_upper, in_lower = (lanes >= at) & (lanes < mid), (lanes >= mid) & (lanes < mid + PB)
        minus_upper = jnp.where(lanes == at + rows, -1.0, 0.0)
        minus_lower = jnp.where(lanes == mid + rows, -1.0, 0.0)
        cols = columns_of(upper, at, width)
        factors = columns_of(lower, at, width)
        first = whole_of(eliminate(cols, parts_of(jnp.where(in_upper, minus_upper, upper), width), width))
        backs = columns_of(first, mid, width)
        rest = less(jnp.where(in_upper, 0.0, lower), factors, first, width)
        cols = columns_of(rest, mid, width)
        second = whole_of(eliminate(cols, parts_of(jnp.where(in_lower, minus_lower, rest), width), width))
        first = less(jnp.where(in_lower, 0.0, first), backs, second, width)
        fresh = jnp.concatenate([first, second], axis=0)
        both = in_upper | in_lower
        source = jnp.concatenate([jnp.where(both, minus_upper, upper), jnp.where(both, minus_lower, lower)], axis=0)
        kept = jnp.where((whole >= at) & (whole < at + 2 * PB), 0.0, s_ref[...])
        s_ref[...] = kept - cross(source, fresh)
        s_ref[pl.ds(at, 2 * PB), :] = fresh
        return carry

    start = 0
    for end, action in between:
        lax.fori_loop(start, end, step, 0)
        action()
        start = end
    lax.fori_loop(start, steps, step, 0)


def dot(a, b):
    return jnp.dot(a, b, preferred_element_type=F32)


def full_dot(a, b):
    return jnp.dot(a, b, precision=lax.Precision.HIGHEST, preferred_element_type=F32)


def kernel(nz, nj, t_hbm, bc_hbm, fa_ref, fb_ref,
           t_f32, t_hi, t_lo, w_hi, w_lo, b_all, b_sib, c_v, c_pad, c_turn, gram_c,
           gram, g1, g1_sum, g2, g2_sum, g3, inverse, system,
           tot, sib, comb, landed, own, m_all, total_b, tot_b, h_land,
           t_sem, in_sem, a_s, a_r, s_s, s_r, g1_s, g1_r, g2_s, g2_r, g3_s, g3_r, g4_s, g4_r,
           c1_s, c1_r, c2_s, c2_r, e1_s, e1_r, e2_s, e2_r, h_s, h_r):
    z, p = lax.axis_index("ia"), lax.axis_index("ja")
    q, c = p // 2, p % 2
    nq = nj // 2
    per, rank = own.shape
    layers, high, wide = t_hbm.shape
    half = rank // 2
    other = p + 1 - 2 * c

    def send(src, dst, s_sem, r_sem, to):
        return pltpu.make_async_remote_copy(
            src_ref=src, dst_ref=dst, send_sem=s_sem, recv_sem=r_sem, device_id=to, device_id_type=MESH
        )

    def arrived(ref, sem):
        pltpu.make_async_copy(ref, ref, sem).wait()

    def each(n, body):
        lax.fori_loop(0, n, lambda s, carry: (body(s), carry)[1], 0)

    def round_z(body):
        each(nz - 1, lambda s: body((z + 1 + (s + nz // 2 - 1) % (nz - 1)) % nz))

    def round_half(n, body):
        each(nz // 2 - 1, lambda s: body(n * (nz // 2) + (z + 1 + s) % (nz // 2)))

    def round_q(body):
        far = (nq // 2 + nq // 8 - 1) % (nq - 1)
        each(nq - 1, lambda s: body((q + 1 + (s + far) % (nq - 1)) % nq))

    barrier = pltpu.get_barrier_semaphore()
    round_q(lambda to: pl.semaphore_signal(barrier, inc=1, device_id=(z, 2 * to + c), device_id_type=MESH))
    round_z(lambda to: pl.semaphore_signal(barrier, inc=1, device_id=(to, p), device_id_type=MESH))
    pl.semaphore_signal(barrier, inc=1, device_id=(z, other), device_id_type=MESH)

    b_copy = pltpu.make_async_copy(bc_hbm.at[pl.ds(0, per)], b_all.at[z], in_sem.at[0])
    c_copy = pltpu.make_async_copy(bc_hbm.at[pl.ds(per, layers)], c_v, in_sem.at[1])
    b_copy.start()
    c_copy.start()
    t_copies = [pltpu.make_async_copy(t_hbm.at[k], t_f32.at[k], t_sem.at[k]) for k in range(layers)]
    for copy in t_copies:
        copy.start()

    def g1_copy(t, to, slot):
        return send(gram.at[t, to], g1.at[t, slot], g1_s.at[t], g1_r.at[t], (z, 2 * to + c))

    def g2_copy(t, to, slot):
        return send(g1_sum.at[t], g2.at[t, slot], g2_s.at[t], g2_r.at[t], (to, p))

    def g3_copy(t, to, slot):
        return send(g2_sum.at[t], g3.at[t, c, slot], g3_s.at[t], g3_r.at[t], (z, 2 * to + c))

    def g4_copy(t, side):
        return send(g3.at[t, side], g3.at[t, side], g4_s.at[t], g4_r.at[t], (z, other))

    def gram_1(t, mine, twin):
        at = pl.multiple_of(c * half, half)
        left = jnp.concatenate([mine[:, pl.ds(at, half)], twin[:, pl.ds(at, half)]], axis=0)
        right = jnp.concatenate([mine[...], twin[...]], axis=0)
        value = cross(left, right).reshape(nq, half // nq, rank)
        gram[t] = value
        round_q(lambda to: g1_copy(t, to, q).start())
        g1[t, q] = gram[t, q]

    def gram_2(t):
        arrived(g1.at[t, pl.ds(0, nq - 1)], g1_r.at[t])
        total = g1[t, 0]
        for s in range(1, nq):
            total = total + g1[t, s]
        g1_sum[t] = total
        round_z(lambda to: g2_copy(t, to, z).start())
        g2[t, z] = total

    def gram_3(t):
        arrived(g2.at[t, pl.ds(0, nz - 1)], g2_r.at[t])
        total = g2[t, 0]
        for s in range(1, nz):
            total = total + g2[t, s]
        g2_sum[t] = total
        round_q(lambda to: g3_copy(t, to, q).start())
        g3[t, c, q] = total

    def gram_4(t):
        arrived(g3.at[t, 0, pl.ds(0, nq - 1)], g3_r.at[t])
        g4_copy(t, c).start()

    def gram_5(t):
        g4_copy(t, 1 - c).wait_recv()
        return g3[t].reshape(rank, rank)

    def system_of(value):
        rows = lax.broadcasted_iota(jnp.int32, (rank, rank), 0)
        lanes = lax.broadcasted_iota(jnp.int32, (rank, rank), 1)
        return gram_c[...] * value + jnp.where(rows == lanes, RIDGE, 0.0)

    def s_copy():
        return send(b_all.at[z], b_sib, s_s.at[0], s_r.at[0], (z, other))

    def a_copy(to, slot, which):
        return send(b_all.at[z], b_all.at[slot], a_s.at[0], a_r.at[which], (to, p))

    b_copy.wait()
    c_copy.wait()
    pl.semaphore_wait(barrier, nq - 1 + nz - 1 + 1)
    s_copy().start()
    round_half(z // (nz // 2), lambda to: a_copy(to, z, 0).start())
    each(nz // 2, lambda s: a_copy((1 - z // (nz // 2)) * (nz // 2) + (z + s) % (nz // 2), z, 1).start())
    s_copy().wait_recv()
    gram_1(0, b_all.at[z], b_sib)

    c_pad[...] = jnp.zeros_like(c_pad)
    c_pad[0:layers, :] = c_v[...]
    gram_c[...] = cross(c_pad[0:16, :], c_pad[0:16, :])
    c_turn[...] = c_pad[...].T

    hw = wide // 2
    sw = layers * hw
    strip = min(256, high)
    for k in range(layers):
        t_copies[k].wait()

        def convert(s, k=k):
            at = pl.multiple_of(s * strip, strip)
            hi, lo = split2(t_f32[k, pl.ds(at, strip), :])
            for n in range(2):
                to = n * sw + k * hw
                t_hi[pl.ds(at, strip), to : to + hw] = hi[:, n * hw : (n + 1) * hw]
                t_lo[pl.ds(at, strip), to : to + hw] = lo[:, n * hw : (n + 1) * hw]

        each(high // strip, convert)

    near = z // (nz // 2)

    def weights(n):
        block = b_all[pl.ds(n * (nz // 2), nz // 2)].reshape(hw, rank)
        for k in range(layers):
            hi, lo = split2(block * c_v[k : k + 1, :])
            at = pl.multiple_of(n * sw + k * hw, hw)
            w_hi[pl.ds(at, hw), :] = hi
            w_lo[pl.ds(at, hw), :] = lo

    def product(n, x):
        size = high // CHUNKS
        at, to = pl.multiple_of(x * size, size), pl.multiple_of(n * sw, sw)
        th, tl = t_hi[pl.ds(at, size), pl.ds(to, sw)], t_lo[pl.ds(at, size), pl.ds(to, sw)]
        wh, wl = w_hi[pl.ds(to, sw), :], w_lo[pl.ds(to, sw), :]
        return (dot(th, wh) + dot(tl, wh) + dot(th, wl)).reshape(nq // CHUNKS, 2, per, rank)

    if nz // 2 > 1:
        arrived(b_all.at[pl.ds(0, nz // 2 - 1)], a_r.at[0])
    weights(near)

    def first(x):
        tot[pl.ds(x * (nq // CHUNKS), nq // CHUNKS)] = product(near, x)

    each(CHUNKS, first)
    gram_2(0)
    arrived(b_all.at[pl.ds(0, nz // 2)], a_r.at[1])
    weights(1 - near)

    group = nq // CHUNKS

    def c1_copy(chip):
        return send(tot.at[chip, 1 - c], sib.at[chip], c1_s.at[0], c1_r.at[chip // group], (z, other))

    def c2_copy(to, slot):
        return send(comb.at[to], landed.at[slot], c2_s.at[0], c2_r.at[0], (z, 2 * to + c))

    def chunk_of(s):
        return (q // group + 1 + s) % CHUNKS

    def multiply(s):
        x = chunk_of(s)
        tot[pl.ds(x * group, group)] += product(1 - near, x)
        each(group, lambda i: c1_copy(x * group + i).start())

    def merge(s):
        x = chunk_of(s)

        arrived(sib.at[pl.ds(0, group)], c1_r.at[x])

        def one(i):
            chip = x * group + i
            value = tot[chip, c] + sib[chip]

            @pl.when(chip != q)
            def _():
                comb[chip] = value
                c2_copy(chip, q).start()

            @pl.when(chip == q)
            def _():
                landed[q] = value

        each(group, one)

    multiply(0)

    def go(s):
        multiply(s + 1)
        merge(s)

    each(CHUNKS - 1, go)
    gram_3(0)
    merge(CHUNKS - 1)

    def e1_copy(to):
        return send(own, m_all.at[p], e1_s.at[0], e1_r.at[q // group], (z, to))

    def twin_copy():
        return send(own, m_all.at[p], e1_s.at[1], e1_r.at[CHUNKS], (z, other))

    def e2_copy(slot, x):
        return send(m_all.at[slot], m_all.at[slot], e2_s.at[0], e2_r.at[x], (z, other))

    def moments_a():
        arrived(landed.at[pl.ds(0, nq - 1)], c2_r.at[0])
        moments = landed[0]
        for s in range(1, nq):
            moments = moments + landed[s]
        own[...] = moments
        twin_copy().start()
        m_all[p] = moments

    def share_moments():
        twin_copy().wait_recv()
        gram_1(1, own, m_all.at[other])
        round_q(lambda to: e1_copy(2 * to + c).start())

    moments_a()
    share_moments()
    gram_4(0)
    inverse[...] = system_of(gram_5(0))
    sweep(inverse, ((MIDDLE, lambda: gram_2(1)),))

    def group_of(s):
        return (q // group + s + s // 2 - 2 * (s // 3)) % CHUNKS

    def landing(s, sem):
        @pl.when(s == 0)
        def _():
            if group > 1:
                arrived(m_all.at[pl.ds(0, group - 1)], sem)

        @pl.when(s != 0)
        def _():
            arrived(m_all.at[pl.ds(0, group)], sem)

    def forward(s):
        x = group_of(s)
        landing(s, e1_r.at[x])

        def one(i):
            chip = x * group + i

            @pl.when(chip != q)
            def _():
                e2_copy(2 * chip + c, x).start()

        each(group, one)

    def back(s):
        x = group_of(s)
        landing(s, e2_r.at[x])
        size = high // CHUNKS
        at = pl.multiple_of(x * size, size)
        block = m_all[pl.ds(x * 2 * group, 2 * group)].reshape(size, rank)
        mh, ml = split2(block)
        ih, il = split2(inverse[...])
        ah, al = split2(-(dot(mh, ih) + dot(ml, ih) + dot(mh, il)).T)
        for n in range(2):
            part = total_b[n]
            for m in range(layers // 2):
                to = n * sw + m * wide
                th, tl = t_hi[pl.ds(at, size), to : to + wide], t_lo[pl.ds(at, size), to : to + wide]
                value = dot(ah, th) + dot(al, th) + dot(ah, tl)
                part = part + value[:, 0:hw] * c_turn[:, 2 * m : 2 * m + 1]
                part = part + value[:, hw:wide] * c_turn[:, 2 * m + 1 : 2 * m + 2]
            total_b[n] = part

    total_b[...] = jnp.zeros_like(total_b)
    forward(0)

    def go_back(s):
        forward(s + 1)
        back(s)

        @pl.when(s == 0)
        def _():
            gram_3(1)

    each(CHUNKS - 1, go_back)
    back(CHUNKS - 1)

    for n in range(2):
        tot_b[n * (nz // 2) : (n + 1) * (nz // 2)] = total_b[n].T.reshape(nz // 2, per, rank)

    def h_copy(to, slot):
        return send(tot_b.at[to], h_land.at[slot], h_s.at[0], h_r.at[0], (to, p))

    round_z(lambda to: h_copy(to, z).start())
    gram_4(1)
    fa_ref[...] = -full_dot(own[...], inverse[...])
    h_land[z] = tot_b[z]

    system[...] = full_dot(inverse[...], gram_5(1))
    system[...] = system_of(full_dot(system[...], inverse[...]))
    sweep(system)

    arrived(h_land.at[pl.ds(0, nz - 1)], h_r.at[0])
    moments = h_land[0]
    for s in range(1, nz):
        moments = moments + h_land[s]
    fb_ref[...] = -full_dot(moments, system[...])

    s_copy().wait_send()
    arrived(b_all.at[pl.ds(0, nz - 1)], a_s.at[0])
    arrived(h_land.at[pl.ds(0, nz - 1)], h_s.at[0])
    for t in range(2):
        arrived(g1.at[t, pl.ds(0, nq - 1)], g1_s.at[t])
        arrived(g2.at[t, pl.ds(0, nz - 1)], g2_s.at[t])
        arrived(g3.at[t, 0, pl.ds(0, nq - 1)], g3_s.at[t])
        g4_copy(t, c).wait_send()
    arrived(sib, c1_s.at[0])
    arrived(landed.at[pl.ds(0, nq - 1)], c2_s.at[0])
    arrived(m_all.at[pl.ds(0, nq - 1)], e1_s.at[0])
    twin_copy().wait_send()
    arrived(m_all.at[pl.ds(0, nq - 1)], e2_s.at[0])


def solution(mesh):
    nz, nj = mesh.shape["ia"], mesh.shape["ja"]
    nq = nj // 2

    def local(tensor, factor_b, factor_c):
        layers, high, wide = tensor.shape
        per, rank = factor_b.shape
        slab = rank // nj
        vm = pltpu.VMEM
        sem = lambda *shape: pltpu.SemaphoreType.DMA(shape)
        out = jax.ShapeDtypeStruct((per, rank), F32)
        whole = pl.BlockSpec(memory_space=pltpu.VMEM)
        anywhere = pl.BlockSpec(memory_space=pltpu.HBM)
        return pl.pallas_call(
            functools.partial(kernel, nz, nj),
            out_shape=(out, out),
            in_specs=[anywhere] * 2,
            out_specs=(whole, whole),
            scratch_shapes=[
                vm((layers, high, wide), F32),
                vm((high, layers * wide), BF16), vm((high, layers * wide), BF16),
                vm((layers * wide, rank), BF16), vm((layers * wide, rank), BF16),
                vm((nz, per, rank), F32), vm((per, rank), F32), vm((layers, rank), F32),
                vm((128, rank), F32), vm((rank, 128), F32), vm((rank, rank), F32),
                vm((2, nq, slab, rank), F32), vm((2, nq, slab, rank), F32), vm((2, slab, rank), F32),
                vm((2, nz, slab, rank), F32), vm((2, slab, rank), F32), vm((2, 2, nq, slab, rank), F32),
                vm((rank, rank), F32), vm((rank, rank), F32),
                vm((nq, 2, per, rank), F32), vm((nq, per, rank), F32), vm((nq, per, rank), F32),
                vm((nq, per, rank), F32), vm((per, rank), F32), vm((nj, per, rank), F32),
                vm((2, rank, wide // 2), F32),
                vm((nz, per, rank), F32), vm((nz, per, rank), F32),
                sem(layers), sem(2), sem(1), sem(2), sem(1), sem(1),
                sem(2), sem(2), sem(2), sem(2), sem(2), sem(2), sem(2), sem(2),
                sem(1), sem(CHUNKS), sem(1), sem(1), sem(2), sem(CHUNKS + 1), sem(1), sem(CHUNKS), sem(1), sem(1),
            ],
            compiler_params=pltpu.CompilerParams(
                collective_id=0, has_side_effects=True, vmem_limit_bytes=48 * 1024 * 1024
            ),
            cost_estimate=pl.CostEstimate(
                flops=4 * layers * high * wide * rank, bytes_accessed=4 * layers * high * wide, transcendentals=0
            ),
        )(tensor, jnp.concatenate([factor_b, factor_c], axis=0))

    in_specs = (P(None, "ia", "ja"), P(("ja", "ia"), None), P())
    out_specs = (P(("ia", "ja"), None), P(("ja", "ia"), None))
    return jax.shard_map(local, mesh=mesh, in_specs=in_specs, out_specs=out_specs, check_vma=False)
```

```python
import functools

import jax
import jax.numpy as jnp
from jax import lax
from jax.experimental import pallas as pl
from jax.experimental.pallas import tpu as pltpu
from jax.sharding import PartitionSpec as P

RIDGE = 0.001
MESH = pl.DeviceIdType.MESH
F32 = jnp.float32
BF16 = jnp.bfloat16
PB = 16
CHUNKS = 4
MIDDLE = 6


def split2(x):
    high = x.astype(BF16)
    return high, (x - high.astype(F32)).astype(BF16)


def split3(x):
    high = x.astype(BF16)
    rest = x - high.astype(F32)
    mid = rest.astype(BF16)
    return high, mid, (rest - mid.astype(F32)).astype(BF16)


def cross(left, right):
    lh, lm, ll = split3(left)
    rh, rm, rl = split3(right)
    a = jnp.concatenate([lh, lh, lm, lh, lm, ll], axis=0)
    b = jnp.concatenate([rh, rm, rh, rl, rm, rh], axis=0)
    return lax.dot_general(a, b, (((0,), (0,)), ((), ())), preferred_element_type=F32)


def row_of(block, at):
    return jnp.broadcast_to(block[at : at + 1, :], block.shape)


def eliminate(cols, panel, width):
    row = lax.broadcasted_iota(jnp.int32, (8, width), 0)
    halves = range(PB // 8)
    for j in range(0, PB, 2):
        h, jj = j // 8, j % 8
        u0, u1 = cols[j], cols[j + 1]
        first, second = row == jj, row == jj + 1
        pair = first | second
        a, b, d = row_of(u0[h], jj), row_of(u0[h], jj + 1), row_of(u1[h], jj + 1)
        scale = 1.0 / (a * d - b * b)
        w0 = [d * u0[g] - b * u1[g] for g in halves]
        w1 = [a * u1[g] - b * u0[g] for g in halves]
        w0[h] = jnp.where(first, -d, jnp.where(second, b, w0[h]))
        w1[h] = jnp.where(first, b, jnp.where(second, -a, w1[h]))

        def step(target):
            q0, q1 = row_of(target[h], jj), row_of(target[h], jj + 1)
            base = [jnp.where(pair, 0.0, target[g]) if g == h else target[g] for g in halves]
            return [base[g] - scale * (w0[g] * q0 + w1[g] * q1) for g in halves]

        cols = [step(col) if l > j + 1 else None for l, col in enumerate(cols)]
        panel = [step(part) for part in panel]
    return panel


def columns_of(panel, at, width):
    lanes = lax.broadcasted_iota(jnp.int32, panel.shape, 1)
    cols = []
    for l in range(PB):
        col = jnp.sum(jnp.where(lanes == at + l, panel, 0.0), axis=1, keepdims=True)
        col = jnp.broadcast_to(col, (PB, width))
        cols.append([col[8 * g : 8 * g + 8] for g in range(PB // 8)])
    return cols


def parts_of(panel, width):
    return [
        [panel[8 * g : 8 * g + 8, w * width : (w + 1) * width] for g in range(PB // 8)]
        for w in range(panel.shape[1] // width)
    ]


def whole_of(parts):
    return jnp.concatenate([jnp.concatenate(part, axis=0) for part in parts], axis=1)


def less(panel, factors, fresh, width):
    parts = parts_of(panel, width)
    for l in range(PB):
        for w, part in enumerate(parts):
            line = jnp.broadcast_to(fresh[l : l + 1, w * width : (w + 1) * width], (8, width))
            for g in range(PB // 8):
                part[g] = part[g] - factors[l][g] * line
    return whole_of(parts)


def sweep(s_ref, between=()):
    size = s_ref.shape[0]
    steps = size // (2 * PB)
    lanes = lax.broadcasted_iota(jnp.int32, (PB, size), 1)
    rows = lax.broadcasted_iota(jnp.int32, (PB, size), 0)
    whole = lax.broadcasted_iota(jnp.int32, (size, size), 1)
    width = 128

    def step(k, carry):
        at = pl.multiple_of(k * 2 * PB, 2 * PB)
        mid = at + PB
        upper, lower = s_ref[pl.ds(at, PB), :], s_ref[pl.ds(pl.multiple_of(mid, PB), PB), :]
        in_upper, in_lower = (lanes >= at) & (lanes < mid), (lanes >= mid) & (lanes < mid + PB)
        minus_upper = jnp.where(lanes == at + rows, -1.0, 0.0)
        minus_lower = jnp.where(lanes == mid + rows, -1.0, 0.0)
        cols = columns_of(upper, at, width)
        factors = columns_of(lower, at, width)
        first = whole_of(eliminate(cols, parts_of(jnp.where(in_upper, minus_upper, upper), width), width))
        backs = columns_of(first, mid, width)
        rest = less(jnp.where(in_upper, 0.0, lower), factors, first, width)
        cols = columns_of(rest, mid, width)
        second = whole_of(eliminate(cols, parts_of(jnp.where(in_lower, minus_lower, rest), width), width))
        first = less(jnp.where(in_lower, 0.0, first), backs, second, width)
        fresh = jnp.concatenate([first, second], axis=0)
        both = in_upper | in_lower
        source = jnp.concatenate([jnp.where(both, minus_upper, upper), jnp.where(both, minus_lower, lower)], axis=0)
        kept = jnp.where((whole >= at) & (whole < at + 2 * PB), 0.0, s_ref[...])
        s_ref[...] = kept - cross(source, fresh)
        s_ref[pl.ds(at, 2 * PB), :] = fresh
        return carry

    start = 0
    for end, action in between:
        lax.fori_loop(start, end, step, 0)
        action()
        start = end
    lax.fori_loop(start, steps, step, 0)


def dot(a, b):
    return jnp.dot(a, b, preferred_element_type=F32)


def full_dot(a, b):
    return jnp.dot(a, b, precision=lax.Precision.HIGHEST, preferred_element_type=F32)


def kernel(nz, nj, t_hbm, bc_hbm, fa_ref, fb_ref,
           t_f32, t_hi, t_lo, w_hi, w_lo, b_all, b_sib, c_v, c_pad, c_turn, gram_c,
           gram, g1, g1_sum, g2, g2_sum, g3, inverse, system,
           tot, sib, comb, landed, own, m_all, total_b, tot_b, h_land,
           t_sem, in_sem, a_s, a_r, s_s, s_r, g1_s, g1_r, g2_s, g2_r, g3_s, g3_r, g4_s, g4_r,
           c1_s, c1_r, c2_s, c2_r, e1_s, e1_r, e2_s, e2_r, h_s, h_r):
    z, p = lax.axis_index("ia"), lax.axis_index("ja")
    q, c = p // 2, p % 2
    nq = nj // 2
    per, rank = own.shape
    layers, high, wide = t_hbm.shape
    half = rank // 2
    other = p + 1 - 2 * c

    def send(src, dst, s_sem, r_sem, to):
        return pltpu.make_async_remote_copy(
            src_ref=src, dst_ref=dst, send_sem=s_sem, recv_sem=r_sem, device_id=to, device_id_type=MESH
        )

    def arrived(ref, sem):
        pltpu.make_async_copy(ref, ref, sem).wait()

    def each(n, body):
        lax.fori_loop(0, n, lambda s, carry: (body(s), carry)[1], 0)

    def round_z(body):
        for s in range(nz - 1):
            body((z + 1 + (s + nz // 2 - 1) % (nz - 1)) % nz)

    def round_half(n, body):
        each(nz // 2 - 1, lambda s: body(n * (nz // 2) + (z + 1 + s) % (nz // 2)))

    def round_q(body):
        far = (nq // 2 + nq // 8 - 1) % (nq - 1)
        for s in range(nq - 1):
            body((q + 1 + (s + far) % (nq - 1)) % nq)

    barrier = pltpu.get_barrier_semaphore()
    round_q(lambda to: pl.semaphore_signal(barrier, inc=1, device_id=(z, 2 * to + c), device_id_type=MESH))
    round_z(lambda to: pl.semaphore_signal(barrier, inc=1, device_id=(to, p), device_id_type=MESH))
    pl.semaphore_signal(barrier, inc=1, device_id=(z, other), device_id_type=MESH)

    b_copy = pltpu.make_async_copy(bc_hbm.at[pl.ds(0, per)], b_all.at[z], in_sem.at[0])
    c_copy = pltpu.make_async_copy(bc_hbm.at[pl.ds(per, layers)], c_v, in_sem.at[1])
    b_copy.start()
    c_copy.start()
    t_copies = [pltpu.make_async_copy(t_hbm.at[k], t_f32.at[k], t_sem.at[k]) for k in range(layers)]
    for copy in t_copies:
        copy.start()

    def g1_copy(t, to, slot):
        return send(gram.at[t, to], g1.at[t, slot], g1_s.at[t], g1_r.at[t], (z, 2 * to + c))

    def g2_copy(t, to, slot):
        return send(g1_sum.at[t], g2.at[t, slot], g2_s.at[t], g2_r.at[t], (to, p))

    def g3_copy(t, to, slot):
        return send(g2_sum.at[t], g3.at[t, c, slot], g3_s.at[t], g3_r.at[t], (z, 2 * to + c))

    def g4_copy(t, side):
        return send(g3.at[t, side], g3.at[t, side], g4_s.at[t], g4_r.at[t], (z, other))

    def gram_1(t, mine, twin):
        at = pl.multiple_of(c * half, half)
        left = jnp.concatenate([mine[:, pl.ds(at, half)], twin[:, pl.ds(at, half)]], axis=0)
        right = jnp.concatenate([mine[...], twin[...]], axis=0)
        value = cross(left, right).reshape(nq, half // nq, rank)
        gram[t] = value
        round_q(lambda to: g1_copy(t, to, q).start())
        g1[t, q] = gram[t, q]

    def gram_2(t):
        arrived(g1.at[t, pl.ds(0, nq - 1)], g1_r.at[t])
        total = g1[t, 0]
        for s in range(1, nq):
            total = total + g1[t, s]
        g1_sum[t] = total
        round_z(lambda to: g2_copy(t, to, z).start())
        g2[t, z] = total

    def gram_3(t):
        arrived(g2.at[t, pl.ds(0, nz - 1)], g2_r.at[t])
        total = g2[t, 0]
        for s in range(1, nz):
            total = total + g2[t, s]
        g2_sum[t] = total
        round_q(lambda to: g3_copy(t, to, q).start())
        g3[t, c, q] = total

    def gram_4(t):
        arrived(g3.at[t, 0, pl.ds(0, nq - 1)], g3_r.at[t])
        g4_copy(t, c).start()

    def gram_5(t):
        g4_copy(t, 1 - c).wait_recv()
        return g3[t].reshape(rank, rank)

    def system_of(value):
        rows = lax.broadcasted_iota(jnp.int32, (rank, rank), 0)
        lanes = lax.broadcasted_iota(jnp.int32, (rank, rank), 1)
        return gram_c[...] * value + jnp.where(rows == lanes, RIDGE, 0.0)

    def s_copy():
        return send(b_all.at[z], b_sib, s_s.at[0], s_r.at[0], (z, other))

    def a_copy(to, slot, which):
        return send(b_all.at[z], b_all.at[slot], a_s.at[0], a_r.at[which], (to, p))

    b_copy.wait()
    c_copy.wait()
    pl.semaphore_wait(barrier, nq - 1 + nz - 1 + 1)
    s_copy().start()
    round_half(z // (nz // 2), lambda to: a_copy(to, z, 0).start())
    each(nz // 2, lambda s: a_copy((1 - z // (nz // 2)) * (nz // 2) + (z + s) % (nz // 2), z, 1).start())
    s_copy().wait_recv()
    gram_1(0, b_all.at[z], b_sib)

    c_pad[...] = jnp.zeros_like(c_pad)
    c_pad[0:layers, :] = c_v[...]
    gram_c[...] = cross(c_pad[0:16, :], c_pad[0:16, :])
    c_turn[...] = c_pad[...].T

    hw = wide // 2
    sw = layers * hw
    strip = min(256, high)
    for k in range(layers):
        t_copies[k].wait()

        def convert(s, k=k):
            at = pl.multiple_of(s * strip, strip)
            hi, lo = split2(t_f32[k, pl.ds(at, strip), :])
            for n in range(2):
                to = n * sw + k * hw
                t_hi[pl.ds(at, strip), to : to + hw] = hi[:, n * hw : (n + 1) * hw]
                t_lo[pl.ds(at, strip), to : to + hw] = lo[:, n * hw : (n + 1) * hw]

        each(high // strip, convert)

    near = z // (nz // 2)

    def weights(n):
        block = b_all[pl.ds(n * (nz // 2), nz // 2)].reshape(hw, rank)
        for k in range(layers):
            hi, lo = split2(block * c_v[k : k + 1, :])
            at = pl.multiple_of(n * sw + k * hw, hw)
            w_hi[pl.ds(at, hw), :] = hi
            w_lo[pl.ds(at, hw), :] = lo

    def product(n, x):
        size = high // CHUNKS
        at, to = pl.multiple_of(x * size, size), pl.multiple_of(n * sw, sw)
        th, tl = t_hi[pl.ds(at, size), pl.ds(to, sw)], t_lo[pl.ds(at, size), pl.ds(to, sw)]
        wh, wl = w_hi[pl.ds(to, sw), :], w_lo[pl.ds(to, sw), :]
        return (dot(th, wh) + dot(tl, wh) + dot(th, wl)).reshape(nq // CHUNKS, 2, per, rank)

    if nz // 2 > 1:
        arrived(b_all.at[pl.ds(0, nz // 2 - 1)], a_r.at[0])
    weights(near)

    def first(x):
        tot[pl.ds(x * (nq // CHUNKS), nq // CHUNKS)] = product(near, x)

    each(CHUNKS, first)
    gram_2(0)
    arrived(b_all.at[pl.ds(0, nz // 2)], a_r.at[1])
    weights(1 - near)

    group = nq // CHUNKS

    def c1_copy(chip):
        return send(tot.at[chip, 1 - c], sib.at[chip], c1_s.at[0], c1_r.at[chip // group], (z, other))

    def c2_copy(to, slot):
        return send(comb.at[to], landed.at[slot], c2_s.at[0], c2_r.at[0], (z, 2 * to + c))

    def chunk_of(s):
        return (q // group + 1 + s) % CHUNKS

    def multiply(s):
        x = chunk_of(s)
        tot[pl.ds(x * group, group)] += product(1 - near, x)
        each(group, lambda i: c1_copy(x * group + i).start())

    def merge(s):
        x = chunk_of(s)

        arrived(sib.at[pl.ds(0, group)], c1_r.at[x])

        def one(i):
            chip = x * group + i
            value = tot[chip, c] + sib[chip]

            @pl.when(chip != q)
            def _():
                comb[chip] = value
                c2_copy(chip, q).start()

            @pl.when(chip == q)
            def _():
                landed[q] = value

        each(group, one)

    multiply(0)

    def go(s):
        multiply(s + 1)
        merge(s)

    each(CHUNKS - 1, go)
    gram_3(0)
    merge(CHUNKS - 1)

    def e1_copy(to):
        return send(own, m_all.at[p], e1_s.at[0], e1_r.at[q // group], (z, to))

    def twin_copy():
        return send(own, m_all.at[p], e1_s.at[1], e1_r.at[CHUNKS], (z, other))

    def e2_copy(slot, x):
        return send(m_all.at[slot], m_all.at[slot], e2_s.at[0], e2_r.at[x], (z, other))

    def moments_a():
        arrived(landed.at[pl.ds(0, nq - 1)], c2_r.at[0])
        moments = landed[0]
        for s in range(1, nq):
            moments = moments + landed[s]
        own[...] = moments
        twin_copy().start()
        m_all[p] = moments

    def share_moments():
        twin_copy().wait_recv()
        gram_1(1, own, m_all.at[other])
        round_q(lambda to: e1_copy(2 * to + c).start())

    moments_a()
    gram_4(0)
    share_moments()
    inverse[...] = system_of(gram_5(0))
    sweep(inverse, ((MIDDLE, lambda: gram_2(1)),))

    def group_of(s):
        return (q // group + s + s // 2 - 2 * (s // 3)) % CHUNKS

    def landing(s, sem):
        @pl.when(s == 0)
        def _():
            if group > 1:
                arrived(m_all.at[pl.ds(0, group - 1)], sem)

        @pl.when(s != 0)
        def _():
            arrived(m_all.at[pl.ds(0, group)], sem)

    def forward(s):
        x = group_of(s)
        landing(s, e1_r.at[x])

        def one(i):
            chip = x * group + i

            @pl.when(chip != q)
            def _():
                e2_copy(2 * chip + c, x).start()

        each(group, one)

    def back(s):
        x = group_of(s)
        landing(s, e2_r.at[x])
        size = high // CHUNKS
        at = pl.multiple_of(x * size, size)
        block = m_all[pl.ds(x * 2 * group, 2 * group)].reshape(size, rank)
        mh, ml = split2(block)
        ih, il = split2(inverse[...])
        ah, al = split2(-(dot(mh, ih) + dot(ml, ih) + dot(mh, il)).T)
        for n in range(2):
            part = total_b[n]
            for m in range(layers // 2):
                to = n * sw + m * wide
                th, tl = t_hi[pl.ds(at, size), to : to + wide], t_lo[pl.ds(at, size), to : to + wide]
                value = dot(ah, th) + dot(al, th) + dot(ah, tl)
                part = part + value[:, 0:hw] * c_turn[:, 2 * m : 2 * m + 1]
                part = part + value[:, hw:wide] * c_turn[:, 2 * m + 1 : 2 * m + 2]
            total_b[n] = part

    total_b[...] = jnp.zeros_like(total_b)
    forward(0)

    def go_back(s):
        forward(s + 1)
        back(s)

        @pl.when(s == 0)
        def _():
            gram_3(1)

    each(CHUNKS - 1, go_back)
    back(CHUNKS - 1)

    for n in range(2):
        tot_b[n * (nz // 2) : (n + 1) * (nz // 2)] = total_b[n].T.reshape(nz // 2, per, rank)

    def h_copy(to, slot):
        return send(tot_b.at[to], h_land.at[slot], h_s.at[0], h_r.at[0], (to, p))

    round_z(lambda to: h_copy(to, z).start())
    gram_4(1)
    fa_ref[...] = -full_dot(own[...], inverse[...])
    h_land[z] = tot_b[z]

    system[...] = full_dot(inverse[...], gram_5(1))
    system[...] = system_of(full_dot(system[...], inverse[...]))
    sweep(system)

    arrived(h_land.at[pl.ds(0, nz - 1)], h_r.at[0])
    moments = h_land[0]
    for s in range(1, nz):
        moments = moments + h_land[s]
    fb_ref[...] = -full_dot(moments, system[...])

    s_copy().wait_send()
    arrived(b_all.at[pl.ds(0, nz - 1)], a_s.at[0])
    arrived(h_land.at[pl.ds(0, nz - 1)], h_s.at[0])
    for t in range(2):
        arrived(g1.at[t, pl.ds(0, nq - 1)], g1_s.at[t])
        arrived(g2.at[t, pl.ds(0, nz - 1)], g2_s.at[t])
        arrived(g3.at[t, 0, pl.ds(0, nq - 1)], g3_s.at[t])
        g4_copy(t, c).wait_send()
    arrived(sib, c1_s.at[0])
    arrived(landed.at[pl.ds(0, nq - 1)], c2_s.at[0])
    arrived(m_all.at[pl.ds(0, nq - 1)], e1_s.at[0])
    twin_copy().wait_send()
    arrived(m_all.at[pl.ds(0, nq - 1)], e2_s.at[0])


def solution(mesh):
    nz, nj = mesh.shape["ia"], mesh.shape["ja"]
    nq = nj // 2

    def local(tensor, factor_b, factor_c):
        layers, high, wide = tensor.shape
        per, rank = factor_b.shape
        slab = rank // nj
        vm = pltpu.VMEM
        sem = lambda *shape: pltpu.SemaphoreType.DMA(shape)
        out = jax.ShapeDtypeStruct((per, rank), F32)
        whole = pl.BlockSpec(memory_space=pltpu.VMEM)
        anywhere = pl.BlockSpec(memory_space=pltpu.HBM)
        return pl.pallas_call(
            functools.partial(kernel, nz, nj),
            out_shape=(out, out),
            in_specs=[anywhere] * 2,
            out_specs=(whole, whole),
            scratch_shapes=[
                vm((layers, high, wide), F32),
                vm((high, layers * wide), BF16), vm((high, layers * wide), BF16),
                vm((layers * wide, rank), BF16), vm((layers * wide, rank), BF16),
                vm((nz, per, rank), F32), vm((per, rank), F32), vm((layers, rank), F32),
                vm((128, rank), F32), vm((rank, 128), F32), vm((rank, rank), F32),
                vm((2, nq, slab, rank), F32), vm((2, nq, slab, rank), F32), vm((2, slab, rank), F32),
                vm((2, nz, slab, rank), F32), vm((2, slab, rank), F32), vm((2, 2, nq, slab, rank), F32),
                vm((rank, rank), F32), vm((rank, rank), F32),
                vm((nq, 2, per, rank), F32), vm((nq, per, rank), F32), vm((nq, per, rank), F32),
                vm((nq, per, rank), F32), vm((per, rank), F32), vm((nj, per, rank), F32),
                vm((2, rank, wide // 2), F32),
                vm((nz, per, rank), F32), vm((nz, per, rank), F32),
                sem(layers), sem(2), sem(1), sem(2), sem(1), sem(1),
                sem(2), sem(2), sem(2), sem(2), sem(2), sem(2), sem(2), sem(2),
                sem(1), sem(CHUNKS), sem(1), sem(1), sem(2), sem(CHUNKS + 1), sem(1), sem(CHUNKS), sem(1), sem(1),
            ],
            compiler_params=pltpu.CompilerParams(
                collective_id=0, has_side_effects=True, vmem_limit_bytes=48 * 1024 * 1024
            ),
            cost_estimate=pl.CostEstimate(
                flops=4 * layers * high * wide * rank, bytes_accessed=4 * layers * high * wide, transcendentals=0
            ),
        )(tensor, jnp.concatenate([factor_b, factor_c], axis=0))

    in_specs = (P(None, "ia", "ja"), P(("ja", "ia"), None), P())
    out_specs = (P(("ia", "ja"), None), P(("ja", "ia"), None))
    return jax.shard_map(local, mesh=mesh, in_specs=in_specs, out_specs=out_specs, check_vma=False)
```

```python
import functools

import jax
import jax.numpy as jnp
from jax import lax
from jax.experimental import pallas as pl
from jax.experimental.pallas import tpu as pltpu
from jax.sharding import PartitionSpec as P

RIDGE = 0.001
MESH = pl.DeviceIdType.MESH
F32 = jnp.float32
BF16 = jnp.bfloat16
PB = 16
CHUNKS = 4
MIDDLE = 6


def split2(x):
    high = x.astype(BF16)
    return high, (x - high.astype(F32)).astype(BF16)


def split3(x):
    high = x.astype(BF16)
    rest = x - high.astype(F32)
    mid = rest.astype(BF16)
    return high, mid, (rest - mid.astype(F32)).astype(BF16)


def cross(left, right):
    lh, lm, ll = split3(left)
    rh, rm, rl = split3(right)
    a = jnp.concatenate([lh, lh, lm, lh, lm, ll], axis=0)
    b = jnp.concatenate([rh, rm, rh, rl, rm, rh], axis=0)
    return lax.dot_general(a, b, (((0,), (0,)), ((), ())), preferred_element_type=F32)


def row_of(block, at):
    return jnp.broadcast_to(block[at : at + 1, :], block.shape)


def eliminate(cols, panel, width):
    row = lax.broadcasted_iota(jnp.int32, (8, width), 0)
    halves = range(PB // 8)
    for j in range(0, PB, 2):
        h, jj = j // 8, j % 8
        u0, u1 = cols[j], cols[j + 1]
        first, second = row == jj, row == jj + 1
        pair = first | second
        a, b, d = row_of(u0[h], jj), row_of(u0[h], jj + 1), row_of(u1[h], jj + 1)
        scale = 1.0 / (a * d - b * b)
        w0 = [d * u0[g] - b * u1[g] for g in halves]
        w1 = [a * u1[g] - b * u0[g] for g in halves]
        w0[h] = jnp.where(first, -d, jnp.where(second, b, w0[h]))
        w1[h] = jnp.where(first, b, jnp.where(second, -a, w1[h]))

        def step(target):
            q0, q1 = row_of(target[h], jj), row_of(target[h], jj + 1)
            base = [jnp.where(pair, 0.0, target[g]) if g == h else target[g] for g in halves]
            return [base[g] - scale * (w0[g] * q0 + w1[g] * q1) for g in halves]

        cols = [step(col) if l > j + 1 else None for l, col in enumerate(cols)]
        panel = [step(part) for part in panel]
    return panel


def columns_of(panel, at, width):
    lanes = lax.broadcasted_iota(jnp.int32, panel.shape, 1)
    cols = []
    for l in range(PB):
        col = jnp.sum(jnp.where(lanes == at + l, panel, 0.0), axis=1, keepdims=True)
        col = jnp.broadcast_to(col, (PB, width))
        cols.append([col[8 * g : 8 * g + 8] for g in range(PB // 8)])
    return cols


def parts_of(panel, width):
    return [
        [panel[8 * g : 8 * g + 8, w * width : (w + 1) * width] for g in range(PB // 8)]
        for w in range(panel.shape[1] // width)
    ]


def whole_of(parts):
    return jnp.concatenate([jnp.concatenate(part, axis=0) for part in parts], axis=1)


def less(panel, factors, fresh, width):
    parts = parts_of(panel, width)
    for l in range(PB):
        for w, part in enumerate(parts):
            line = jnp.broadcast_to(fresh[l : l + 1, w * width : (w + 1) * width], (8, width))
            for g in range(PB // 8):
                part[g] = part[g] - factors[l][g] * line
    return whole_of(parts)


def sweep(s_ref, between=()):
    size = s_ref.shape[0]
    steps = size // (2 * PB)
    lanes = lax.broadcasted_iota(jnp.int32, (PB, size), 1)
    rows = lax.broadcasted_iota(jnp.int32, (PB, size), 0)
    whole = lax.broadcasted_iota(jnp.int32, (size, size), 1)
    width = 128

    def step(k, carry):
        at = pl.multiple_of(k * 2 * PB, 2 * PB)
        mid = at + PB
        upper, lower = s_ref[pl.ds(at, PB), :], s_ref[pl.ds(pl.multiple_of(mid, PB), PB), :]
        in_upper, in_lower = (lanes >= at) & (lanes < mid), (lanes >= mid) & (lanes < mid + PB)
        minus_upper = jnp.where(lanes == at + rows, -1.0, 0.0)
        minus_lower = jnp.where(lanes == mid + rows, -1.0, 0.0)
        cols = columns_of(upper, at, width)
        factors = columns_of(lower, at, width)
        first = whole_of(eliminate(cols, parts_of(jnp.where(in_upper, minus_upper, upper), width), width))
        backs = columns_of(first, mid, width)
        rest = less(jnp.where(in_upper, 0.0, lower), factors, first, width)
        cols = columns_of(rest, mid, width)
        second = whole_of(eliminate(cols, parts_of(jnp.where(in_lower, minus_lower, rest), width), width))
        first = less(jnp.where(in_lower, 0.0, first), backs, second, width)
        fresh = jnp.concatenate([first, second], axis=0)
        both = in_upper | in_lower
        source = jnp.concatenate([jnp.where(both, minus_upper, upper), jnp.where(both, minus_lower, lower)], axis=0)
        kept = jnp.where((whole >= at) & (whole < at + 2 * PB), 0.0, s_ref[...])
        s_ref[...] = kept - cross(source, fresh)
        s_ref[pl.ds(at, 2 * PB), :] = fresh
        return carry

    start = 0
    for end, action in between:
        lax.fori_loop(start, end, step, 0)
        action()
        start = end
    lax.fori_loop(start, steps, step, 0)


def dot(a, b):
    return jnp.dot(a, b, preferred_element_type=F32)


def full_dot(a, b):
    return jnp.dot(a, b, precision=lax.Precision.HIGHEST, preferred_element_type=F32)


def kernel(nz, nj, t_hbm, bc_hbm, fa_ref, fb_ref,
           t_f32, t_hi, t_lo, w_hi, w_lo, b_all, b_sib, c_v, c_pad, c_turn, gram_c,
           gram, g1, g1_sum, g2, g2_sum, g3, inverse, system,
           tot, sib, comb, landed, own, m_all, total_b, tot_b, h_land,
           t_sem, in_sem, a_s, a_r, s_s, s_r, g1_s, g1_r, g2_s, g2_r, g3_s, g3_r, g4_s, g4_r,
           c1_s, c1_r, c2_s, c2_r, e1_s, e1_r, e2_s, e2_r, h_s, h_r):
    z, p = lax.axis_index("ia"), lax.axis_index("ja")
    q, c = p // 2, p % 2
    nq = nj // 2
    per, rank = own.shape
    layers, high, wide = t_hbm.shape
    half = rank // 2
    other = p + 1 - 2 * c

    def send(src, dst, s_sem, r_sem, to):
        return pltpu.make_async_remote_copy(
            src_ref=src, dst_ref=dst, send_sem=s_sem, recv_sem=r_sem, device_id=to, device_id_type=MESH
        )

    def arrived(ref, sem):
        pltpu.make_async_copy(ref, ref, sem).wait()

    def each(n, body):
        lax.fori_loop(0, n, lambda s, carry: (body(s), carry)[1], 0)

    def round_z(body):
        for s in range(nz - 1):
            body((z + 1 + (s + nz // 2 - 1) % (nz - 1)) % nz)

    def round_half(n, body):
        each(nz // 2 - 1, lambda s: body(n * (nz // 2) + (z + 1 + s) % (nz // 2)))

    def round_q(body):
        far = (nq // 2 + nq // 8 - 1) % (nq - 1)
        for s in range(nq - 1):
            body((q + 1 + (s + far) % (nq - 1)) % nq)

    barrier = pltpu.get_barrier_semaphore()
    round_q(lambda to: pl.semaphore_signal(barrier, inc=1, device_id=(z, 2 * to + c), device_id_type=MESH))
    round_z(lambda to: pl.semaphore_signal(barrier, inc=1, device_id=(to, p), device_id_type=MESH))
    pl.semaphore_signal(barrier, inc=1, device_id=(z, other), device_id_type=MESH)

    b_copy = pltpu.make_async_copy(bc_hbm.at[pl.ds(0, per)], b_all.at[z], in_sem.at[0])
    c_copy = pltpu.make_async_copy(bc_hbm.at[pl.ds(per, layers)], c_v, in_sem.at[1])
    b_copy.start()
    c_copy.start()
    t_copies = [pltpu.make_async_copy(t_hbm.at[k], t_f32.at[k], t_sem.at[k]) for k in range(layers)]
    for copy in t_copies:
        copy.start()

    def g1_copy(t, to, slot):
        return send(gram.at[t, to], g1.at[t, slot], g1_s.at[t], g1_r.at[t], (z, 2 * to + c))

    def g2_copy(t, to, slot):
        return send(g1_sum.at[t], g2.at[t, slot], g2_s.at[t], g2_r.at[t], (to, p))

    def g3_copy(t, to, slot):
        return send(g2_sum.at[t], g3.at[t, c, slot], g3_s.at[t], g3_r.at[t], (z, 2 * to + c))

    def g4_copy(t, side):
        return send(g3.at[t, side], g3.at[t, side], g4_s.at[t], g4_r.at[t], (z, other))

    def gram_1(t, mine, twin):
        at = pl.multiple_of(c * half, half)
        left = jnp.concatenate([mine[:, pl.ds(at, half)], twin[:, pl.ds(at, half)]], axis=0)
        right = jnp.concatenate([mine[...], twin[...]], axis=0)
        value = cross(left, right).reshape(nq, half // nq, rank)
        gram[t] = value
        round_q(lambda to: g1_copy(t, to, q).start())
        g1[t, q] = gram[t, q]

    def gram_2(t):
        arrived(g1.at[t, pl.ds(0, nq - 1)], g1_r.at[t])
        total = g1[t, 0]
        for s in range(1, nq):
            total = total + g1[t, s]
        g1_sum[t] = total
        round_z(lambda to: g2_copy(t, to, z).start())
        g2[t, z] = total

    def gram_3(t):
        arrived(g2.at[t, pl.ds(0, nz - 1)], g2_r.at[t])
        total = g2[t, 0]
        for s in range(1, nz):
            total = total + g2[t, s]
        g2_sum[t] = total
        round_q(lambda to: g3_copy(t, to, q).start())
        g3[t, c, q] = total

    def gram_4(t):
        arrived(g3.at[t, 0, pl.ds(0, nq - 1)], g3_r.at[t])
        g4_copy(t, c).start()

    def gram_5(t):
        g4_copy(t, 1 - c).wait_recv()
        return g3[t].reshape(rank, rank)

    def system_of(value):
        rows = lax.broadcasted_iota(jnp.int32, (rank, rank), 0)
        lanes = lax.broadcasted_iota(jnp.int32, (rank, rank), 1)
        return gram_c[...] * value + jnp.where(rows == lanes, RIDGE, 0.0)

    def s_copy():
        return send(b_all.at[z], b_sib, s_s.at[0], s_r.at[0], (z, other))

    def a_copy(to, slot, which):
        return send(b_all.at[z], b_all.at[slot], a_s.at[0], a_r.at[which], (to, p))

    b_copy.wait()
    c_copy.wait()
    pl.semaphore_wait(barrier, nq - 1 + nz - 1 + 1)
    s_copy().start()
    round_half(z // (nz // 2), lambda to: a_copy(to, z, 0).start())
    each(nz // 2, lambda s: a_copy((1 - z // (nz // 2)) * (nz // 2) + (z + s) % (nz // 2), z, 1).start())
    s_copy().wait_recv()
    gram_1(0, b_all.at[z], b_sib)

    c_pad[...] = jnp.zeros_like(c_pad)
    c_pad[0:layers, :] = c_v[...]
    gram_c[...] = cross(c_pad[0:16, :], c_pad[0:16, :])
    c_turn[...] = c_pad[...].T

    hw = wide // 2
    sw = layers * hw
    strip = min(256, high)
    for k in range(layers):
        t_copies[k].wait()

        def convert(s, k=k):
            at = pl.multiple_of(s * strip, strip)
            hi, lo = split2(t_f32[k, pl.ds(at, strip), :])
            for n in range(2):
                to = n * sw + k * hw
                t_hi[pl.ds(at, strip), to : to + hw] = hi[:, n * hw : (n + 1) * hw]
                t_lo[pl.ds(at, strip), to : to + hw] = lo[:, n * hw : (n + 1) * hw]

        each(high // strip, convert)

    near = z // (nz // 2)

    def weights(n):
        block = b_all[pl.ds(n * (nz // 2), nz // 2)].reshape(hw, rank)
        for k in range(layers):
            hi, lo = split2(block * c_v[k : k + 1, :])
            at = pl.multiple_of(n * sw + k * hw, hw)
            w_hi[pl.ds(at, hw), :] = hi
            w_lo[pl.ds(at, hw), :] = lo

    def product(n, x):
        size = high // CHUNKS
        at, to = pl.multiple_of(x * size, size), pl.multiple_of(n * sw, sw)
        th, tl = t_hi[pl.ds(at, size), pl.ds(to, sw)], t_lo[pl.ds(at, size), pl.ds(to, sw)]
        wh, wl = w_hi[pl.ds(to, sw), :], w_lo[pl.ds(to, sw), :]
        return (dot(th, wh) + dot(tl, wh) + dot(th, wl)).reshape(nq // CHUNKS, 2, per, rank)

    if nz // 2 > 1:
        arrived(b_all.at[pl.ds(0, nz // 2 - 1)], a_r.at[0])
    weights(near)

    def first(x):
        tot[pl.ds(x * (nq // CHUNKS), nq // CHUNKS)] = product(near, x)

    each(CHUNKS, first)
    gram_2(0)
    arrived(b_all.at[pl.ds(0, nz // 2)], a_r.at[1])
    weights(1 - near)

    group = nq // CHUNKS

    def c1_copy(chip):
        return send(tot.at[chip, 1 - c], sib.at[chip], c1_s.at[0], c1_r.at[chip // group], (z, other))

    def c2_copy(to, slot):
        return send(comb.at[to], landed.at[slot], c2_s.at[0], c2_r.at[0], (z, 2 * to + c))

    def chunk_of(s):
        return (q // group + 1 + s) % CHUNKS

    def multiply(s):
        x = chunk_of(s)
        tot[pl.ds(x * group, group)] += product(1 - near, x)
        each(group, lambda i: c1_copy(x * group + i).start())

    def merge(s):
        x = chunk_of(s)

        arrived(sib.at[pl.ds(0, group)], c1_r.at[x])

        def one(i):
            chip = x * group + i
            value = tot[chip, c] + sib[chip]

            @pl.when(chip != q)
            def _():
                comb[chip] = value
                c2_copy(chip, q).start()

            @pl.when(chip == q)
            def _():
                landed[q] = value

        each(group, one)

    multiply(0)

    def go(s):
        multiply(s + 1)
        merge(s)

    each(CHUNKS - 1, go)
    gram_3(0)
    merge(CHUNKS - 1)

    def e1_copy(to):
        return send(own, m_all.at[p], e1_s.at[0], e1_r.at[q // group], (z, to))

    def twin_copy():
        return send(own, m_all.at[p], e1_s.at[1], e1_r.at[CHUNKS], (z, other))

    def e2_copy(slot, x):
        return send(m_all.at[slot], m_all.at[slot], e2_s.at[0], e2_r.at[x], (z, other))

    def moments_a():
        arrived(landed.at[pl.ds(0, nq - 1)], c2_r.at[0])
        moments = landed[0]
        for s in range(1, nq):
            moments = moments + landed[s]
        own[...] = moments
        twin_copy().start()
        m_all[p] = moments

    def share_moments():
        twin_copy().wait_recv()
        gram_1(1, own, m_all.at[other])
        round_q(lambda to: e1_copy(2 * to + c).start())

    moments_a()
    gram_4(0)
    share_moments()
    inverse[...] = system_of(gram_5(0))
    sweep(inverse, ((MIDDLE, lambda: gram_2(1)),))

    def group_of(s):
        return (q // group + s + s // 2 - 2 * (s // 3)) % CHUNKS

    def landing(s, sem):
        @pl.when(s == 0)
        def _():
            if group > 1:
                arrived(m_all.at[pl.ds(0, group - 1)], sem)

        @pl.when(s != 0)
        def _():
            arrived(m_all.at[pl.ds(0, group)], sem)

    def forward(s):
        x = group_of(s)
        landing(s, e1_r.at[x])

        def one(i):
            chip = x * group + i

            @pl.when(chip != q)
            def _():
                e2_copy(2 * chip + c, x).start()

        each(group, one)

    def back(s):
        x = group_of(s)
        landing(s, e2_r.at[x])
        size = high // CHUNKS
        at = pl.multiple_of(x * size, size)
        block = m_all[pl.ds(x * 2 * group, 2 * group)].reshape(size, rank)
        mh, ml = split2(block)
        ih, il = split2(inverse[...])
        ah, al = split2(-(dot(mh, ih) + dot(ml, ih) + dot(mh, il)).T)
        for n in range(2):
            part = total_b[n]
            for m in range(layers // 2):
                to = n * sw + m * wide
                th, tl = t_hi[pl.ds(at, size), to : to + wide], t_lo[pl.ds(at, size), to : to + wide]
                value = dot(ah, th) + dot(al, th) + dot(ah, tl)
                part = part + value[:, 0:hw] * c_turn[:, 2 * m : 2 * m + 1]
                part = part + value[:, hw:wide] * c_turn[:, 2 * m + 1 : 2 * m + 2]
            total_b[n] = part

    total_b[...] = jnp.zeros_like(total_b)
    forward(0)

    def go_back(s):
        forward(s + 1)

        @pl.when(s == 0)
        def _():
            gram_3(1)

        back(s)

    each(CHUNKS - 1, go_back)
    back(CHUNKS - 1)

    for n in range(2):
        tot_b[n * (nz // 2) : (n + 1) * (nz // 2)] = total_b[n].T.reshape(nz // 2, per, rank)

    def h_copy(to, slot):
        return send(tot_b.at[to], h_land.at[slot], h_s.at[0], h_r.at[0], (to, p))

    round_z(lambda to: h_copy(to, z).start())
    gram_4(1)
    fa_ref[...] = -full_dot(own[...], inverse[...])
    h_land[z] = tot_b[z]

    system[...] = full_dot(inverse[...], gram_5(1))
    system[...] = system_of(full_dot(system[...], inverse[...]))
    sweep(system)

    arrived(h_land.at[pl.ds(0, nz - 1)], h_r.at[0])
    moments = h_land[0]
    for s in range(1, nz):
        moments = moments + h_land[s]
    fb_ref[...] = -full_dot(moments, system[...])

    s_copy().wait_send()
    arrived(b_all.at[pl.ds(0, nz - 1)], a_s.at[0])
    arrived(h_land.at[pl.ds(0, nz - 1)], h_s.at[0])
    for t in range(2):
        arrived(g1.at[t, pl.ds(0, nq - 1)], g1_s.at[t])
        arrived(g2.at[t, pl.ds(0, nz - 1)], g2_s.at[t])
        arrived(g3.at[t, 0, pl.ds(0, nq - 1)], g3_s.at[t])
        g4_copy(t, c).wait_send()
    arrived(sib, c1_s.at[0])
    arrived(landed.at[pl.ds(0, nq - 1)], c2_s.at[0])
    arrived(m_all.at[pl.ds(0, nq - 1)], e1_s.at[0])
    twin_copy().wait_send()
    arrived(m_all.at[pl.ds(0, nq - 1)], e2_s.at[0])


def solution(mesh):
    nz, nj = mesh.shape["ia"], mesh.shape["ja"]
    nq = nj // 2

    def local(tensor, factor_b, factor_c):
        layers, high, wide = tensor.shape
        per, rank = factor_b.shape
        slab = rank // nj
        vm = pltpu.VMEM
        sem = lambda *shape: pltpu.SemaphoreType.DMA(shape)
        out = jax.ShapeDtypeStruct((per, rank), F32)
        whole = pl.BlockSpec(memory_space=pltpu.VMEM)
        anywhere = pl.BlockSpec(memory_space=pltpu.HBM)
        return pl.pallas_call(
            functools.partial(kernel, nz, nj),
            out_shape=(out, out),
            in_specs=[anywhere] * 2,
            out_specs=(whole, whole),
            scratch_shapes=[
                vm((layers, high, wide), F32),
                vm((high, layers * wide), BF16), vm((high, layers * wide), BF16),
                vm((layers * wide, rank), BF16), vm((layers * wide, rank), BF16),
                vm((nz, per, rank), F32), vm((per, rank), F32), vm((layers, rank), F32),
                vm((128, rank), F32), vm((rank, 128), F32), vm((rank, rank), F32),
                vm((2, nq, slab, rank), F32), vm((2, nq, slab, rank), F32), vm((2, slab, rank), F32),
                vm((2, nz, slab, rank), F32), vm((2, slab, rank), F32), vm((2, 2, nq, slab, rank), F32),
                vm((rank, rank), F32), vm((rank, rank), F32),
                vm((nq, 2, per, rank), F32), vm((nq, per, rank), F32), vm((nq, per, rank), F32),
                vm((nq, per, rank), F32), vm((per, rank), F32), vm((nj, per, rank), F32),
                vm((2, rank, wide // 2), F32),
                vm((nz, per, rank), F32), vm((nz, per, rank), F32),
                sem(layers), sem(2), sem(1), sem(2), sem(1), sem(1),
                sem(2), sem(2), sem(2), sem(2), sem(2), sem(2), sem(2), sem(2),
                sem(1), sem(CHUNKS), sem(1), sem(1), sem(2), sem(CHUNKS + 1), sem(1), sem(CHUNKS), sem(1), sem(1),
            ],
            compiler_params=pltpu.CompilerParams(
                collective_id=0, has_side_effects=True, vmem_limit_bytes=48 * 1024 * 1024
            ),
            cost_estimate=pl.CostEstimate(
                flops=4 * layers * high * wide * rank, bytes_accessed=4 * layers * high * wide, transcendentals=0
            ),
        )(tensor, jnp.concatenate([factor_b, factor_c], axis=0))

    in_specs = (P(None, "ia", "ja"), P(("ja", "ia"), None), P())
    out_specs = (P(("ia", "ja"), None), P(("ja", "ia"), None))
    return jax.shard_map(local, mesh=mesh, in_specs=in_specs, out_specs=out_specs, check_vma=False)
```
